256 devices in a mesh: stator: 64 (over z, y, core), axial: 4 (over x).
Axes of the slice: x: 4, y: 4, z: 8, core: 2. Of those that a mesh axis runs over, the one named last changes fastest.
Arguments:
- coeffs: float32 [32, 262144], P(None, ('stator', 'axial')), may hold values from -6 to 6
- elem_edge: int32 [6, 262144], P(None, ('stator', 'axial')), may hold values from 0 to 1151
- curl_map: float32 [3, 6, 262144], P(None, None, ('stator', 'axial')), may hold values from -1.8 to 1.8
- jacobian: bfloat16 [6, 32, 262144], P(None, None, ('stator', 'axial')), may hold values from -4 to 10, as said below
- flux_fwd: bfloat16 [3, 32, 262144], P(None, None, ('stator', 'axial')), may hold values from -6 to 6
- density: float32 [262144], P(('stator', 'axial')), may hold values from 0.05 to 1
- mortar: float32 [128, 128], replicated, may hold values from -0.5 to 0.5
- gap_peer: int32 [32768, 1], P(('stator', 'axial')), may hold values from 0 to 63; in each aligned block of 128 rows (0 to 127, 128 to 255, ...) at most 4 rows name the same one
- gap_block: int32 [32768], P(('stator', 'axial')), may hold values from 0 to 1
Outputs:
- adjoint: float32 [32, 262144], P(None, ('stator', 'axial'))
- density_grad: float32 [262144], P(('stator', 'axial'))
The draws below stay inside these ranges and needn't reach their ends.
Inputs may be any that keep to these rules, and one draw needn't show every extreme that they name: `elem_edge`: each entry indexes the device's own 1024 edges followed by the first 128 edges of the next axial slab. `gap_peer`: row s * 4 + b of one device names the stator index whose face meets rotor face block b at sample s; at most 4 rows of one device name the same index, and exactly 4 for some index. `jacobian`: each sample's six components form a symmetric matrix with positive diagonal; each off-diagonal entry is at most 0.41 times the square root of the product of its two diagonal entries, so the matrix is positive definite.
All inputs are finite; a program needn't handle non-finite values.
Results may differ from the reference program's by a relative error of at most 0.0003.
Values sent between devices are 32-bit elements; how exact they have to be, the bound alone decides.
A program may use at most 64 MiB of HBM per device.

```python
import math
import jax
import jax.numpy as jnp
import numpy as np
from jax import lax

S = 32
EDGE_DEV = 1024
ELEM_DEV = 1024
FACE = 128
GE = 128
GB = 4
QB = 2
CAP = 4
EDGES = 262144
ELEMS = 262144
N_STATOR = 64
N_AXIAL = 4


def draw_jacobian(key, part):
    first_key, second_key = jax.random.split(jax.random.fold_in(key, 17))
    diagonal = jnp.exp(jax.random.uniform(first_key, (3, S, ELEMS), jnp.float32, 0.0, math.log(10.0)))
    spread = jnp.clip(jax.random.normal(second_key, (3, S, ELEMS), jnp.float32) * 0.2, -0.4, 0.4)
    pairs = jnp.stack([jnp.sqrt(diagonal[0] * diagonal[1]), jnp.sqrt(diagonal[0] * diagonal[2]), jnp.sqrt(diagonal[1] * diagonal[2])])
    return jnp.concatenate([diagonal, spread * pairs], 0).astype(jnp.bfloat16)


def place_ends(result, rng, least, high):
    longest = result.shape.index(max(result.shape))
    spots = []
    for shift in (0, 1):
        where = [jax.random.randint(jax.random.fold_in(rng, axis), (), 0, length) for axis, length in enumerate(result.shape)]
        where[longest] = (where[longest] + shift) % result.shape[longest]
        spots.append(tuple(where))
    return result.at[spots[0]].set(least).at[spots[1]].set(high)


def shard_levels(rng, dims, cuts, low, top_value):
    gain = 1.0
    for dim, shards_of in cuts:
        heights = jax.random.uniform(jax.random.fold_in(jax.random.fold_in(rng, 6), dim), (shards_of,), jnp.float32, low / len(cuts), top_value / len(cuts))
        gain = gain * jnp.repeat(jnp.exp(heights), dims[dim] // shards_of).reshape((-1,) + (1,) * (len(dims) - 1 - dim))
    return gain


def assign_block(rng, own, number, rows, count, top, bound, slope):
    sequence = jax.random.permutation(rng, count)
    heavy_load, common = shares(count, rows * top, bound, slope, True), shares(count, rows * top, bound, slope, False)
    places = jnp.arange(count)

    def named(sizes, turn):
        used = int((sizes > 0).sum())
        fixed = max(1, used // 4)
        moved = fixed + (places - fixed + turn * (used - fixed)) % max(1, count - fixed)
        return jnp.zeros((count,), jnp.int32).at[sequence[jnp.where(places < fixed, places, moved)]].set(jnp.asarray(sizes, jnp.int32))

    sizes = jnp.where(number % 4 == 0, named(heavy_load, number // 4), named(common, number - number // 4 - 1))
    mixed = jax.random.permutation(jax.random.fold_in(own, 3), count)
    source_of, taker = mixed[0:count // 2 * 2:2], mixed[1:count // 2 * 2:2]
    margin = jnp.minimum(sizes[source_of] - 1, bound - sizes[taker]) // 2
    margin = jnp.where((source_of == sequence[0]) | (taker == sequence[0]) | (sizes[taker] == 0), 0, jnp.maximum(margin, 0))
    moved = jax.random.randint(jax.random.fold_in(own, 4), (count // 2,), 0, 1 << 20) % (margin + 1)
    sizes = sizes.at[source_of].add(-moved).at[taker].add(moved)
    labels = jnp.searchsorted(jnp.cumsum(sizes), jnp.arange(rows * top), side="right").astype(jnp.int32)
    listing = labels.reshape(top, rows).T
    listing = listing[jax.random.permutation(jax.random.fold_in(own, 1), rows)]
    turn = jax.random.randint(jax.random.fold_in(own, 2), (rows, 1), 0, top)
    return jnp.take_along_axis(listing, (jnp.arange(top)[None, :] + turn) % top, axis=1)


def shares(count, total, most, slope, full):
    weights = [(1 << 20) // math.isqrt(standing ** slope) + 1 for standing in range(1, count + 1)]
    largest = most if full else min(most, max(-(-total // count), total * weights[0] // sum(weights)))
    least = 1 if total - largest >= count - 1 else 0
    counts, surplus = [largest] + [least] * (count - 1), total - largest - least * (count - 1)
    while surplus > 0:
        movable = [i for i in range(1, count) if counts[i] < largest] or [i for i in range(1, count) if counts[i] < most]
        pool, left = sum([weights[i] for i in movable]), surplus
        for i in movable:
            more = min(most - counts[i], max(1, left * weights[i] // pool), surplus)
            counts[i] = counts[i] + more
            surplus = surplus - more
    return np.array(counts)


def bell_draw(rng, dims, deviation, bound, cuts=(), kind=jnp.bfloat16):
    result = deviation * jax.random.normal(rng, dims, jnp.float32)
    if cuts:
        result = result * shard_levels(rng, dims, cuts, -0.22, 0.18)
    return jnp.clip(result, -bound, bound).astype(kind)


def setup_inputs(seed: int = 0) -> dict:
    arg_keys = jax.random.split(jax.random.key(seed), 10)
    coeffs = bell_draw(arg_keys[0], (S, EDGES), 1.0, 6.0, ((1, 256),), jnp.float32)
    elem_edge = place_ends(jax.random.randint(arg_keys[1], (6, ELEMS), 0, EDGE_DEV + FACE), jax.random.fold_in(arg_keys[1], 1), 0, (EDGE_DEV + FACE) - 1).astype(jnp.int32)
    curl_map = bell_draw(arg_keys[2], (3, 6, ELEMS), 0.3, 1.8, ((2, 256),), jnp.float32)
    jacobian = draw_jacobian(jax.random.fold_in(arg_keys[9], 71), 0)
    flux_fwd = bell_draw(arg_keys[4], (3, S, ELEMS), 1.0, 6.0, ((2, 256),))
    density = jnp.clip(0.05 + 0.95 * jax.random.uniform(arg_keys[5], (ELEMS,), jnp.float32) ** shard_levels(arg_keys[5], (ELEMS,), ((0, 256),), -0.2, 0.2), 0.05, 1.0)
    mortar = bell_draw(arg_keys[6], (GE, GE), GE ** -0.5, 0.5, (), jnp.float32)
    gap_peer_keys = jax.random.split(jax.random.fold_in(arg_keys[7], 1), (N_STATOR * N_AXIAL * S * GB) // (S * GB))
    gap_peer_turns = jax.random.permutation(jax.random.fold_in(arg_keys[7], 3), (N_STATOR * N_AXIAL * S * GB) // (S * GB))
    gap_peer = jax.vmap(lambda own, number: assign_block(jax.random.fold_in(arg_keys[7], 2), own, number, S * GB, N_STATOR, 1, CAP, 2))(gap_peer_keys, gap_peer_turns).reshape((N_STATOR * N_AXIAL * S * GB, 1))
    gap_block = place_ends(jax.random.randint(arg_keys[8], (N_STATOR * N_AXIAL * S * GB,), 0, QB), jax.random.fold_in(arg_keys[8], 1), 0, QB - 1).astype(jnp.int32)
    return {"coeffs": coeffs, "elem_edge": elem_edge, "curl_map": curl_map, "jacobian": jacobian, "flux_fwd": flux_fwd, "density": density, "mortar": mortar, "gap_peer": gap_peer, "gap_block": gap_block}


PENALTY = 4.0
SIMP_POWER = 3.0

def dft_table(count):
    rows = jnp.arange(count, dtype=jnp.float32)[:, None]
    index = jnp.arange(count, dtype=jnp.int32)
    harmonic = ((index + 1) // 2).astype(jnp.float32)[None, :]
    is_sine = ((index % 2 == 0) & (index > 0))[None, :]
    angle = 2.0 * math.pi * harmonic * rows / count
    table = jnp.where(is_sine, jnp.sin(angle), jnp.cos(angle))
    return table * jnp.float32(math.sqrt(2.0 / count))

def element_work(extended, elem_edge, curl_map, jacobian, flux_fwd, density):
    samples = extended.shape[0]
    values = extended[:, elem_edge]
    flux_lam = jnp.einsum('cke,ske->cse', curl_map, values, precision=lax.Precision.HIGHEST)
    jac = jacobian.astype(jnp.float32)
    field_h = jnp.stack([jac[0] * flux_lam[0] + jac[3] * flux_lam[1] + jac[4] * flux_lam[2], jac[3] * flux_lam[0] + jac[1] * flux_lam[1] + jac[5] * flux_lam[2], jac[4] * flux_lam[0] + jac[5] * flux_lam[1] + jac[2] * flux_lam[2]])
    element_terms = jnp.einsum('cke,cse->kes', curl_map, field_h, precision=lax.Precision.HIGHEST)
    summed = jax.ops.segment_sum(element_terms.reshape(-1, samples), elem_edge.reshape(-1), num_segments=extended.shape[1])
    energy = lax.optimization_barrier(jnp.sum(flux_lam * flux_fwd.astype(jnp.float32), axis=(0, 1)))
    grad = SIMP_POWER * density * density * energy / samples
    return (summed.T, grad)

def reference(coeffs, elem_edge, curl_map, jacobian, flux_fwd, density, mortar, gap_peer, gap_block):
    devices = N_STATOR * N_AXIAL
    table = dft_table(S)
    in_time = jnp.dot(table, coeffs, precision=lax.Precision.HIGHEST)
    grid = in_time.reshape(S, N_STATOR, N_AXIAL, EDGE_DEV)
    upper_rim = jnp.concatenate([grid[:, :, 1:, :FACE], jnp.zeros((S, N_STATOR, 1, FACE), jnp.float32)], 2)
    extended = jnp.concatenate([grid, upper_rim], 3).transpose(1, 2, 0, 3).reshape(devices, S, EDGE_DEV + FACE)

    def one_device(device):

        def cols(arr):
            return lax.dynamic_slice_in_dim(arr, device * ELEM_DEV, ELEM_DEV, arr.ndim - 1)
        return element_work(extended[device], cols(elem_edge), cols(curl_map), cols(jacobian), cols(flux_fwd), cols(density))
    res_ext, grads = lax.map(one_device, jnp.arange(devices, dtype=jnp.int32))
    res_ext = res_ext.reshape(N_STATOR, N_AXIAL, S, EDGE_DEV + FACE)
    own = res_ext[..., :EDGE_DEV]
    rim = res_ext[..., EDGE_DEV:]
    own = own.at[:, 1:, :, :FACE].add(rim[:, :-1])
    rotor = grid[..., EDGE_DEV - GB * GE:].reshape(S, N_STATOR, N_AXIAL, GB, GE).transpose(1, 2, 0, 3, 4)
    stator = grid[..., FACE:FACE + QB * GE].reshape(S, N_STATOR, N_AXIAL, QB, GE).transpose(1, 2, 0, 3, 4)
    mapped = jnp.einsum('nasqg,gh->nasqh', stator, mortar, precision=lax.Precision.HIGHEST)
    owners = gap_peer[:, 0].reshape(N_STATOR, N_AXIAL, S, GB)
    blocks = gap_block.reshape(N_STATOR, N_AXIAL, S, GB)
    axial_idx = jnp.broadcast_to(jnp.arange(N_AXIAL, dtype=jnp.int32)[None, :, None, None], owners.shape)
    sample_idx = jnp.broadcast_to(jnp.arange(S, dtype=jnp.int32)[None, None, :, None], owners.shape)
    facing = mapped[owners, axial_idx, sample_idx, blocks]
    jumps = rotor - facing
    gathered = jnp.zeros((N_STATOR, N_AXIAL, S, QB, GE), jnp.float32).at[owners, axial_idx, sample_idx, blocks].add(jumps)
    stator_terms = -PENALTY * jnp.einsum('nasqg,hg->nasqh', gathered, mortar, precision=lax.Precision.HIGHEST)
    own = own.at[..., EDGE_DEV - GB * GE:].add(PENALTY * jumps.reshape(N_STATOR, N_AXIAL, S, GB * GE))
    own = own.at[..., FACE:FACE + QB * GE].add(stator_terms.reshape(N_STATOR, N_AXIAL, S, QB * GE))
    residual = own.transpose(2, 0, 1, 3).reshape(S, devices * EDGE_DEV)
    adjoint = jnp.dot(table.T, residual, precision=lax.Precision.HIGHEST)
    return (adjoint, grads.reshape(-1))
```

```python
import functools
import math

import jax
import jax.numpy as jnp
import numpy as np
from jax import lax
from jax.experimental import pallas as pl
from jax.experimental.pallas import tpu as pltpu
from jax.sharding import PartitionSpec as P

GE = 128
GB = 4
QB = 2
CAP = 4
PENALTY = 4.0
SIMP_POWER = 3.0
CHUNK = 256

MESH = pl.DeviceIdType.MESH
F32 = jnp.float32
BF16 = jnp.bfloat16
NN = (((1,), (0,)), ((), ()))
NT = (((1,), (1,)), ((), ()))


def dft_table(count):
    rows = np.arange(count, dtype=np.float64)[:, None]
    index = np.arange(count)
    harmonic = ((index + 1) // 2).astype(np.float64)[None, :]
    is_sine = ((index % 2 == 0) & (index > 0))[None, :]
    angle = 2.0 * math.pi * harmonic * rows / count
    table = np.where(is_sine, np.sin(angle), np.cos(angle))
    return (table * math.sqrt(2.0 / count)).astype(np.float32)


def triple(table):
    high = table.astype(jnp.bfloat16)
    low = (table - high.astype(np.float32)).astype(jnp.bfloat16)
    return np.concatenate([high, high, low], 1)


def split(value):
    high = value.astype(BF16)
    return high, (value - high.astype(F32)).astype(BF16)


def mul(a, b, dims=NN):
    return lax.dot_general(a, b, dims, preferred_element_type=F32)


def table_dot(table, value):
    high, low = split(value)
    return mul(table, jnp.concatenate([high, low, high], 0))


def dot3(a, b, dims=NN):
    a_high, a_low = split(a)
    b_high, b_low = split(b)
    return mul(a_high, b_high, dims) + mul(a_high, b_low, dims) + mul(a_low, b_high, dims)


def side_by_side(value):
    return jnp.concatenate(split(value), 1)


def add_halves(value):
    half = value.shape[1] // 2
    return value[:, :half] + value[:, half:]


def as_bf16(mask):
    return jnp.where(mask, F32(1), F32(0)).astype(BF16)


def iota(shape, dim):
    return lax.broadcasted_iota(jnp.int32, shape, dim)


def kernel(
    stators,
    axials,
    coeffs,
    edge,
    curl,
    jac,
    fwd,
    density,
    mortar,
    packed,
    table,
    table_t,
    adjoint,
    grad,
    upper,
    lower_out,
    lower_in,
    meta,
    sendbuf,
    recvbuf,
    mapped_rows,
    in_time,
    ext,
    hot,
    acc,
    upper_send,
    upper_recv,
    lower_send,
    lower_recv,
    meta_send,
    meta_recv,
    data_send,
    data_recv,
):
    samples, edges = coeffs.shape
    face = edges // 8
    extended = edges + face
    rows = samples * GB
    slots = 2 * CAP
    rotor_start = edges - GB * GE
    me, ax = lax.axis_index("stator"), lax.axis_index("axial")
    above, below = lax.rem(ax + 1, axials), lax.rem(ax + axials - 1, axials)

    barrier = pltpu.get_barrier_semaphore()

    def greet(step, carry):
        peer = lax.rem(me + step, stators)
        pl.semaphore_signal(barrier, inc=1, device_id=(peer, ax), device_id_type=MESH)
        return carry

    for other in (above, below):
        pl.semaphore_signal(barrier, inc=1, device_id=(me, other), device_id_type=MESH)
    lax.fori_loop(1, stators, greet, 0)

    a, b = iota((rows, rows), 0), iota((rows, rows), 1)
    own_order = b == lax.rem(a, samples) * GB + lax.div(a, samples)
    listed = packed[...].astype(F32)
    col = jnp.sum(jnp.where(own_order, listed, 0.0), axis=1, keepdims=True)
    row = jnp.sum(jnp.where(a == b, col, 0.0), axis=0, keepdims=True)
    peer_col, peer_row = jnp.floor(col * 0.5), jnp.floor(row * 0.5)
    same = peer_col == peer_row
    rank_row = jnp.sum(jnp.where(same & (a < b), 1.0, 0.0), axis=0, keepdims=True)
    rank_col = jnp.sum(jnp.where(same & (b < a), 1.0, 0.0), axis=1, keepdims=True)
    slot_row = (peer_row * slots + rank_row).astype(jnp.int32)
    slot_col = (peer_col * slots + rank_col).astype(jnp.int32)
    code_row = (peer_row * CAP + rank_row) * QB + (row - 2.0 * peer_row)
    own_slots = pl.ds(pl.multiple_of(me * slots, slots), slots)
    meta[own_slots, :] = jnp.broadcast_to(code_row, (slots, rows))

    pl.semaphore_wait(barrier, stators - 1 + 2)

    upper_copy = pltpu.make_async_remote_copy(
        src_ref=coeffs.at[:, pl.ds(0, face)],
        dst_ref=upper,
        send_sem=upper_send,
        recv_sem=upper_recv,
        device_id=(me, below),
        device_id_type=MESH,
    )
    upper_copy.start()

    def send_meta(step, carry):
        peer = lax.rem(me + step, stators)
        pltpu.make_async_remote_copy(
            src_ref=meta.at[own_slots, :],
            dst_ref=meta.at[own_slots, :],
            send_sem=meta_send,
            recv_sem=meta_recv,
            device_id=(peer, ax),
            device_id_type=MESH,
        ).start()
        return carry

    lax.fori_loop(1, stators, send_meta, 0)

    in_time[...] = table_dot(table[...], coeffs[...])
    own_high, own_low = split(in_time[...])
    ext[0:samples, 0:edges] = own_high
    ext[samples : 2 * samples, 0:edges] = own_low
    for q in range(QB):
        here = in_time[:, face + q * GE : face + (q + 1) * GE]
        mapped_rows[q * samples : (q + 1) * samples, :] = dot3(here, mortar[...])

    upper_copy.wait()
    inside = jnp.where(ax < axials - 1, F32(1), F32(0))
    rim_high, rim_low = split(table_dot(table[...], upper[...] * inside))
    ext[0:samples, edges:extended] = rim_high
    ext[samples : 2 * samples, edges:extended] = rim_low

    acc[...] = jnp.zeros_like(acc)

    def element_chunk(chunk, carry):
        lanes = pl.ds(pl.multiple_of(chunk * CHUNK, CHUNK), CHUNK)
        sub = iota((extended, CHUNK), 0).astype(jnp.int16)
        named = edge[:, lanes].astype(jnp.int16)
        for m in range(6):
            mask = sub == named[m : m + 1, :]
            hot[:, m * CHUNK : (m + 1) * CHUNK] = jnp.where(mask, BF16(1), BF16(0))
        values = mul(ext[...], hot[...])
        values = values[:samples] + values[samples:]
        maps = curl[:, :, lanes]
        flux = []
        for c in range(3):
            total = None
            for m in range(6):
                term = maps[c, m : m + 1, :] * values[:, m * CHUNK : (m + 1) * CHUNK]
                total = term if total is None else total + term
            flux.append(total)
        j = [jac[k, :, lanes].astype(F32) for k in range(6)]
        field = [
            j[0] * flux[0] + j[3] * flux[1] + j[4] * flux[2],
            j[3] * flux[0] + j[1] * flux[1] + j[5] * flux[2],
            j[4] * flux[0] + j[5] * flux[1] + j[2] * flux[2],
        ]
        energy = sum(flux[c] * fwd[c, :, lanes].astype(F32) for c in range(3))
        energy = jnp.sum(energy, axis=0, keepdims=True)
        dens = density[:, lanes]
        grad[:, lanes] = SIMP_POWER * dens * dens * energy / samples
        highs, lows = [], []
        for m in range(6):
            high, low = split(sum(maps[c, m : m + 1, :] * field[c] for c in range(3)))
            highs.append(high)
            lows.append(low)
        terms = jnp.concatenate([jnp.concatenate(highs, 1), jnp.concatenate(lows, 1)], 0)
        acc[...] += mul(terms, hot[...], NT)
        return carry

    chunks = edges // CHUNK
    lax.fori_loop(0, chunks // 2, element_chunk, 0)

    def all_meta(buf):
        return pltpu.make_async_copy(
            buf.at[pl.ds(0, (stators - 1) * slots), :],
            buf.at[pl.ds(0, (stators - 1) * slots), :],
            meta_recv,
        )

    all_meta(meta).wait()
    every = stators * slots
    place = iota((every, rows), 0)
    rank_here = lax.rem(place, CAP)
    wanted = lax.rem(place, slots) >= CAP
    codes = meta[...]
    mapped = mapped_rows[...]
    hits = [as_bf16(codes == ((me * CAP + rank_here) * QB + q).astype(F32)) for q in range(QB)]
    tiled = [jnp.concatenate([mapped[q * samples : (q + 1) * samples]] * GB, 0) for q in range(QB)]
    facing_rows = add_halves(
        mul(jnp.concatenate(hits, 1), side_by_side(jnp.concatenate(tiled, 0)))
    )
    rotor = jnp.concatenate(
        [in_time[:, rotor_start + b * GE : rotor_start + (b + 1) * GE] for b in range(GB)], 0
    )
    rotor_rows = add_halves(mul(as_bf16(place == slot_row), side_by_side(rotor)))
    sendbuf[...] = rotor_rows + jnp.where(wanted, facing_rows, 0.0)

    def send_data(step, carry):
        peer = lax.rem(me + step, stators)
        pltpu.make_async_remote_copy(
            src_ref=sendbuf.at[pl.ds(pl.multiple_of(peer * slots, slots), slots), :],
            dst_ref=recvbuf.at[own_slots, :],
            send_sem=data_send,
            recv_sem=data_recv,
            device_id=(peer, ax),
            device_id_type=MESH,
        ).start()
        return carry

    lax.fori_loop(1, stators, send_data, 0)
    recvbuf[own_slots, :] = sendbuf[own_slots, :]

    place_t = iota((rows, every), 1)
    codes_t = codes.T
    takers = [as_bf16(place_t == slot_col + CAP)]
    given = lax.rem(place_t, slots) < CAP
    rank_t = lax.rem(place_t, CAP)
    for q in range(QB):
        hit = given & (codes_t == ((me * CAP + rank_t) * QB + q).astype(F32))
        hit = jnp.where(hit, F32(1), F32(0))
        folded = sum(hit[b * samples : (b + 1) * samples] for b in range(GB))
        takers.append(folded.astype(BF16))
    takers = jnp.concatenate(takers, 0)

    lax.fori_loop(chunks // 2, chunks, element_chunk, 0)

    lower_out[...] = acc[:samples, edges:extended] + acc[samples : 2 * samples, edges:extended]
    lower_copy = pltpu.make_async_remote_copy(
        src_ref=lower_out,
        dst_ref=lower_in,
        send_sem=lower_send,
        recv_sem=lower_recv,
        device_id=(me, above),
        device_id_type=MESH,
    )
    lower_copy.start()

    def bulk(buf, sem):
        view = buf.at[pl.ds(0, (stators - 1) * slots), :]
        return pltpu.make_async_copy(view, view, sem)

    bulk(recvbuf, data_recv).wait()
    jumps = recvbuf[...] - jnp.where(wanted, 0.0, facing_rows)
    sums = add_halves(mul(takers, side_by_side(jumps)))
    rotor_term = PENALTY * (rotor - sums[:rows])
    stator_term = -PENALTY * dot3(sums[rows:], mortar[...], NT)
    for b in range(GB):
        lanes = pl.ds(rotor_start + b * GE, GE)
        acc[0:samples, lanes] += rotor_term[b * samples : (b + 1) * samples]
    for q in range(QB):
        lanes = pl.ds(face + q * GE, GE)
        acc[0:samples, lanes] += stator_term[q * samples : (q + 1) * samples]

    lower_copy.wait()
    linked = jnp.where(ax > 0, F32(1), F32(0))
    acc[0:samples, 0:face] += lower_in[...] * linked
    residual = acc[0:samples, 0:edges] + acc[samples : 2 * samples, 0:edges]
    adjoint[...] = table_dot(table_t[...], residual)

    bulk(meta, meta_send).wait()
    bulk(sendbuf, data_send).wait()


def on_device(coeffs, elem_edge, curl_map, jacobian, flux_fwd, density, mortar, gap_peer, gap_block):
    stators, axials = lax.axis_size("stator"), lax.axis_size("axial")
    samples, edges = coeffs.shape
    elements = elem_edge.shape[1]
    face = edges // 8
    rows = samples * GB
    every = stators * 2 * CAP
    table = dft_table(samples)
    packed = gap_peer.reshape(1, rows) * QB + gap_block.reshape(1, rows)
    vmem = pl.BlockSpec(memory_space=pltpu.VMEM)
    adjoint, grad = pl.pallas_call(
        functools.partial(kernel, stators, axials),
        out_shape=(
            jax.ShapeDtypeStruct((samples, edges), F32),
            jax.ShapeDtypeStruct((1, elements), F32),
        ),
        in_specs=[vmem] * 10,
        out_specs=(vmem, vmem),
        scratch_shapes=[
            pltpu.VMEM((samples, face), F32),
            pltpu.VMEM((samples, face), F32),
            pltpu.VMEM((samples, face), F32),
            pltpu.VMEM((every, rows), F32),
            pltpu.VMEM((every, GE), F32),
            pltpu.VMEM((every, GE), F32),
            pltpu.VMEM((samples * QB, GE), F32),
            pltpu.VMEM((samples, edges), F32),
            pltpu.VMEM((2 * samples, edges + face), BF16),
            pltpu.VMEM((edges + face, 6 * CHUNK), BF16),
            pltpu.VMEM((2 * samples, edges + face), F32),
        ]
        + [pltpu.SemaphoreType.DMA] * 8,
        compiler_params=pltpu.CompilerParams(
            collective_id=0, has_side_effects=True, vmem_limit_bytes=48 * 1024 * 1024
        ),
    )(
        coeffs,
        elem_edge,
        curl_map,
        jacobian,
        flux_fwd,
        density.reshape(1, elements),
        mortar,
        packed,
        jnp.asarray(triple(table)),
        jnp.asarray(triple(np.ascontiguousarray(table.T))),
    )
    return adjoint, grad.reshape(elements)


def solution(mesh):
    placed = (
        P(None, ("stator", "axial")),
        P(None, ("stator", "axial")),
        P(None, None, ("stator", "axial")),
        P(None, None, ("stator", "axial")),
        P(None, None, ("stator", "axial")),
        P(("stator", "axial")),
        P(),
        P(("stator", "axial"), None),
        P(("stator", "axial")),
    )
    return jax.shard_map(
        on_device,
        mesh=mesh,
        in_specs=placed,
        out_specs=(P(None, ("stator", "axial")), P(("stator", "axial"))),
        check_vma=False,
    )
```

```python
import functools
import math

import jax
import jax.numpy as jnp
import numpy as np
from jax import lax
from jax.experimental import pallas as pl
from jax.experimental.pallas import tpu as pltpu
from jax.sharding import PartitionSpec as P

GE = 128
GB = 4
QB = 2
CAP = 4
PENALTY = 4.0
SIMP_POWER = 3.0
CHUNK = 256
GROUP = 8

MESH = pl.DeviceIdType.MESH
F32 = jnp.float32
BF16 = jnp.bfloat16
NN = (((1,), (0,)), ((), ()))
NT = (((1,), (1,)), ((), ()))


def dft_table(count):
    rows = np.arange(count, dtype=np.float64)[:, None]
    index = np.arange(count)
    harmonic = ((index + 1) // 2).astype(np.float64)[None, :]
    is_sine = ((index % 2 == 0) & (index > 0))[None, :]
    angle = 2.0 * math.pi * harmonic * rows / count
    table = np.where(is_sine, np.sin(angle), np.cos(angle))
    return (table * math.sqrt(2.0 / count)).astype(np.float32)


def triple(table):
    high = table.astype(jnp.bfloat16)
    low = (table - high.astype(np.float32)).astype(jnp.bfloat16)
    return np.concatenate([high, high, low], 1)


def split(value):
    high = value.astype(BF16)
    return high, (value - high.astype(F32)).astype(BF16)


def mul(a, b, dims=NN):
    return lax.dot_general(a, b, dims, preferred_element_type=F32)


def table_dot(table, value):
    high, low = split(value)
    return mul(table, jnp.concatenate([high, low, high], 0))


def dot3(a, b, dims=NN):
    a_high, a_low = split(a)
    b_high, b_low = split(b)
    return mul(a_high, b_high, dims) + mul(a_high, b_low, dims) + mul(a_low, b_high, dims)


def side_by_side(value):
    return jnp.concatenate(split(value), 1)


def add_halves(value):
    half = value.shape[1] // 2
    return value[:, :half] + value[:, half:]


def as_bf16(mask):
    return jnp.where(mask, F32(1), F32(0)).astype(BF16)


def iota(shape, dim):
    return lax.broadcasted_iota(jnp.int32, shape, dim)


def kernel(
    stators,
    axials,
    coeffs_hbm,
    edge_hbm,
    curl_hbm,
    jac_hbm,
    fwd_hbm,
    density_hbm,
    mortar_hbm,
    peers_hbm,
    blocks_hbm,
    table_hbm,
    table_t_hbm,
    adjoint_hbm,
    grad_hbm,
    coeffs,
    edge,
    curl,
    jac,
    fwd,
    density,
    mortar,
    peers,
    blocks,
    table,
    table_t,
    upper,
    lower_out,
    lower_in,
    code_own,
    codes,
    mapped,
    rotor_out,
    rotor_mid,
    rotor_in,
    reply_out,
    reply_in,
    ext,
    values,
    hot,
    acc,
    adjoint,
    grad,
    load,
    send,
    recv,
    store,
):
    samples, edges = coeffs.shape
    face = edges // 8
    extended = edges + face
    rows = samples * GB
    ring = stators // GROUP
    rotor_start = edges - GB * GE
    me, ax = lax.axis_index("stator"), lax.axis_index("axial")
    z, w = lax.div(me, GROUP), lax.rem(me, GROUP)
    above, below = lax.rem(ax + 1, axials), lax.rem(ax + axials - 1, axials)

    arrivals = []
    for index, (source, target) in enumerate(
        (
            (peers_hbm, peers),
            (blocks_hbm, blocks),
            (coeffs_hbm, coeffs),
            (table_hbm, table),
            (mortar_hbm, mortar),
            (edge_hbm, edge),
            (curl_hbm, curl),
            (jac_hbm, jac),
            (fwd_hbm, fwd),
            (density_hbm, density),
            (table_t_hbm, table_t),
        )
    ):
        arrivals.append(pltpu.make_async_copy(source, target, load.at[index]))
        arrivals[-1].start()

    along_z = sorted(range(1, ring), key=lambda step: -min(step, ring - step))
    along_w = sorted(range(1, GROUP), key=lambda step: -min(step, GROUP - step))
    z_peers = [lax.rem(z + step, ring) for step in along_z]
    w_peers = [lax.rem(w + step, GROUP) for step in along_w]

    barrier = pltpu.get_barrier_semaphore()

    def greet(stator, axial):
        pl.semaphore_signal(barrier, inc=1, device_id=(stator, axial), device_id_type=MESH)

    for other in z_peers:
        greet(other * GROUP + w, ax)
    for other in w_peers:
        greet(z * GROUP + other, ax)
    for other in (above, below):
        greet(me, other)

    def push(source, target, index, stator, axial):
        copy = pltpu.make_async_remote_copy(
            src_ref=source,
            dst_ref=target,
            send_sem=send.at[index],
            recv_sem=recv.at[index],
            device_id=(stator, axial),
            device_id_type=MESH,
        )
        copy.start()
        return copy

    def await_bytes(view, sem):
        pltpu.make_async_copy(view, view, sem).wait()

    arrivals[0].wait()
    arrivals[1].wait()
    a, b = iota((rows, rows), 0), iota((rows, rows), 1)
    own_order = b == lax.rem(a, samples) * GB + lax.div(a, samples)
    listed = (peers[...] * QB + blocks[...]).astype(F32)
    col = jnp.sum(jnp.where(own_order, listed, 0.0), axis=1, keepdims=True)
    row = jnp.sum(jnp.where(a == b, col, 0.0), axis=0, keepdims=True)
    peer_col, peer_row = jnp.floor(col * 0.5), jnp.floor(row * 0.5)
    same = peer_col == peer_row
    rank_row = jnp.sum(jnp.where(same & (a < b), 1.0, 0.0), axis=0, keepdims=True)
    rank_col = jnp.sum(jnp.where(same & (b < a), 1.0, 0.0), axis=1, keepdims=True)

    def slot(peer, rank):
        ring_place = jnp.floor(peer * (1.0 / GROUP))
        group_place = peer - GROUP * ring_place
        return (group_place * (ring * CAP) + ring_place * CAP + rank).astype(jnp.int32)

    slot_row, slot_col = slot(peer_row, rank_row), slot(peer_col, rank_col)
    code_row = (peer_row * CAP + rank_row) * QB + (row - 2.0 * peer_row)
    code_own[...] = jnp.broadcast_to(code_row, (CAP, rows))

    arrivals[2].wait()
    arrivals[3].wait()
    arrivals[4].wait()
    own = table_dot(table[...], coeffs[...])
    ext[:, 0:edges] = own
    slots = stators * CAP
    rotor = jnp.concatenate(
        [own[:, rotor_start + b * GE : rotor_start + (b + 1) * GE] for b in range(GB)], 0
    )
    placed = as_bf16(iota((slots, rows), 0) == slot_row)
    rotor_out[...] = add_halves(mul(placed, side_by_side(rotor))).reshape(rotor_out.shape)
    faces = jnp.concatenate(
        [own[:, face + q * GE : face + (q + 1) * GE] for q in range(QB)], 0
    )
    own_mapped = dot3(faces, mortar[...])
    mapped[w] = own_mapped

    pl.semaphore_wait(barrier, (ring - 1) + (GROUP - 1) + 2)

    upper_copy = push(coeffs.at[:, pl.ds(0, face)], upper, 0, me, below)
    at_me = pl.ds(z * CAP, CAP)
    for other in z_peers:
        push(code_own, codes.at[w, at_me], 1, other * GROUP + w, ax)
    pltpu.make_async_copy(code_own, codes.at[w, at_me], recv.at[1]).start()
    for other in w_peers:
        push(mapped.at[w], mapped.at[w], 2, z * GROUP + other, ax)
    for other in z_peers:
        push(
            rotor_out.at[:, pl.ds(other * CAP, CAP)],
            rotor_mid.at[:, at_me],
            3,
            other * GROUP + w,
            ax,
        )
    pltpu.make_async_copy(rotor_out.at[:, at_me], rotor_mid.at[:, at_me], recv.at[3]).start()

    arrivals[5].wait()

    def pick(lanes, m):
        named = jnp.broadcast_to(edge[m : m + 1, lanes], (samples, GE))
        return named & (GE - 1), lax.shift_right_logical(named, GE.bit_length() - 1)

    def gather_own(part, carry):
        lanes = pl.ds(pl.multiple_of(part * GE, GE), GE)
        for m in range(6):
            low, high = pick(lanes, m)
            found = None
            for k in range(edges // GE):
                here = jnp.take_along_axis(ext[:, k * GE : (k + 1) * GE], low, axis=1)
                found = here if found is None else jnp.where(high == k, here, found)
            values[m, :, lanes] = found
        return carry

    lax.fori_loop(0, edges // GE, gather_own, 0)

    upper_copy.wait_recv()
    inside = jnp.where(ax < axials - 1, F32(1), F32(0))
    ext[:, edges:extended] = table_dot(table[...], upper[...] * inside)
    for index in range(6, 10):
        arrivals[index].wait()
    acc[...] = jnp.zeros_like(acc)

    def element_chunk(chunk, carry):
        lanes = pl.ds(pl.multiple_of(chunk * CHUNK, CHUNK), CHUNK)
        sub = iota((extended, CHUNK), 0).astype(jnp.int16)
        named = edge[:, lanes].astype(jnp.int16)
        for m in range(6):
            mask = sub == named[m : m + 1, :]
            hot[:, m * CHUNK : (m + 1) * CHUNK] = jnp.where(mask, BF16(1), BF16(0))
        found = []
        for m in range(6):
            pieces = []
            for part in range(CHUNK // GE):
                here = pl.ds(pl.multiple_of(chunk * CHUNK + part * GE, GE), GE)
                low, high = pick(here, m)
                rim = jnp.take_along_axis(ext[:, edges:extended], low, axis=1)
                pieces.append(jnp.where(high == edges // GE, rim, values[m, :, here]))
            found.append(jnp.concatenate(pieces, 1))
        maps = curl[:, :, lanes]
        flux = [sum(maps[c, m : m + 1, :] * found[m] for m in range(6)) for c in range(3)]
        j = [jac[k, :, lanes].astype(F32) for k in range(6)]
        field = [
            j[0] * flux[0] + j[3] * flux[1] + j[4] * flux[2],
            j[3] * flux[0] + j[1] * flux[1] + j[5] * flux[2],
            j[4] * flux[0] + j[5] * flux[1] + j[2] * flux[2],
        ]
        energy = sum(flux[c] * fwd[c, :, lanes].astype(F32) for c in range(3))
        energy = jnp.sum(energy, axis=0, keepdims=True)
        dens = density[:, lanes]
        grad[:, lanes] = SIMP_POWER * dens * dens * energy / samples
        highs, lows = [], []
        for m in range(6):
            high, low = split(sum(maps[c, m : m + 1, :] * field[c] for c in range(3)))
            highs.append(high)
            lows.append(low)
        terms = jnp.concatenate([jnp.concatenate(highs, 1), jnp.concatenate(lows, 1)], 0)
        acc[...] += mul(hot[...], terms, NT)
        return carry

    lax.fori_loop(0, edges // CHUNK, element_chunk, 0)
    kept = [pltpu.make_async_copy(grad, grad_hbm, store.at[0])]
    kept[0].start()
    sums = acc[...].T
    sums = sums[:samples] + sums[samples : 2 * samples]
    lower_out[...] = sums[:, edges:extended]
    lower_copy = push(lower_out, lower_in, 4, me, above)

    await_bytes(codes.at[w], recv.at[1])
    for other in w_peers:
        push(codes.at[w], codes.at[w], 5, z * GROUP + other, ax)
    await_bytes(mapped.at[pl.ds(0, GROUP - 1)], recv.at[2])
    asked = codes[w]
    rank = lax.rem(iota((ring * CAP, rows), 0), CAP)

    def by_row(value):
        return jnp.concatenate([value] * GB, 0)

    for other in range(GROUP):
        hits = [
            as_bf16(asked == (((z * GROUP + other) * CAP + rank) * QB + q).astype(F32))
            for q in range(QB)
        ]
        source = [by_row(mapped[other, q * samples : (q + 1) * samples]) for q in range(QB)]
        reply_out[other] = add_halves(
            mul(jnp.concatenate(hits, 1), side_by_side(jnp.concatenate(source, 0)))
        )
    for other in z_peers:
        push(
            reply_out.at[:, pl.ds(other * CAP, CAP)],
            reply_in.at[:, at_me],
            6,
            other * GROUP + w,
            ax,
        )
    pltpu.make_async_copy(reply_out.at[:, at_me], reply_in.at[:, at_me], recv.at[6]).start()

    await_bytes(rotor_mid, recv.at[3])
    for other in w_peers:
        push(rotor_mid.at[other], rotor_in.at[w], 7, z * GROUP + other, ax)
    rotor_in[w] = rotor_mid[w]
    await_bytes(codes.at[pl.ds(0, GROUP - 1)], recv.at[5])
    listed_t = codes[...].reshape(slots, rows).T
    rank_t = lax.rem(iota((rows, slots), 1), CAP)
    takers, counts = [], []
    for q in range(QB):
        hit = listed_t == ((me * CAP + rank_t) * QB + q).astype(F32)
        hit = jnp.where(hit, F32(1), F32(0))
        folded = sum(hit[b * samples : (b + 1) * samples] for b in range(GB))
        takers.append(folded.astype(BF16))
        counts.append(jnp.sum(folded, axis=1, keepdims=True))
    takers, counts = jnp.concatenate(takers, 0), jnp.concatenate(counts, 0)
    await_bytes(rotor_in.at[pl.ds(0, GROUP - 1)], recv.at[7])
    arrived = add_halves(mul(takers, side_by_side(rotor_in[...].reshape(slots, GE))))
    stator_term = -PENALTY * dot3(arrived - counts * mapped[w], mortar[...], NT)

    arrivals[10].wait()
    lower_copy.wait_recv()
    linked = jnp.where(ax > 0, F32(1), F32(0))
    residual = [sums[:, 0:face] + lower_in[...] * linked]
    for q in range(QB):
        here = sums[:, face + q * GE : face + (q + 1) * GE]
        residual.append(here + stator_term[q * samples : (q + 1) * samples])
    residual.append(sums[:, face + QB * GE : rotor_start])
    adjoint[:, 0:rotor_start] = table_dot(table_t[...], jnp.concatenate(residual, 1))
    first, last = pl.ds(0, rotor_start), pl.ds(rotor_start, edges - rotor_start)
    kept.append(
        pltpu.make_async_copy(adjoint.at[:, first], adjoint_hbm.at[:, first], store.at[1])
    )
    kept[1].start()

    chosen = as_bf16(iota((rows, slots), 1) == slot_col)
    await_bytes(reply_in, recv.at[6])
    facing = add_halves(mul(chosen, side_by_side(reply_in[...].reshape(slots, GE))))
    jumps = rotor - facing
    residual = [
        sums[:, rotor_start + b * GE : rotor_start + (b + 1) * GE]
        + PENALTY * jumps[b * samples : (b + 1) * samples]
        for b in range(GB)
    ]
    adjoint[:, rotor_start:edges] = table_dot(table_t[...], jnp.concatenate(residual, 1))

    kept.append(pltpu.make_async_copy(adjoint.at[:, last], adjoint_hbm.at[:, last], store.at[2]))
    kept[2].start()

    upper_copy.wait_send()
    lower_copy.wait_send()
    await_bytes(codes.at[0, pl.ds(0, (ring - 1) * CAP)], send.at[1])
    await_bytes(mapped.at[pl.ds(0, GROUP - 1)], send.at[2])
    await_bytes(rotor_mid.at[:, pl.ds(0, (ring - 1) * CAP)], send.at[3])
    await_bytes(codes.at[pl.ds(0, GROUP - 1)], send.at[5])
    await_bytes(reply_out.at[:, pl.ds(0, (ring - 1) * CAP)], send.at[6])
    await_bytes(rotor_in.at[pl.ds(0, GROUP - 1)], send.at[7])
    for copy in kept:
        copy.wait()


def flush(a, b, c, d):
    c[...] = a[...]
    d[...] = b[...]


def on_device(coeffs, elem_edge, curl_map, jacobian, flux_fwd, density, mortar, gap_peer, gap_block):
    stators, axials = lax.axis_size("stator"), lax.axis_size("axial")
    samples, edges = coeffs.shape
    elements = elem_edge.shape[1]
    face = edges // 8
    rows = samples * GB
    ring = stators // GROUP
    table = dft_table(samples)
    operands = (
        coeffs,
        elem_edge,
        curl_map,
        jacobian,
        flux_fwd,
        density.reshape(1, elements),
        mortar,
        gap_peer.reshape(1, rows),
        gap_block.reshape(1, rows),
        jnp.asarray(triple(table)),
        jnp.asarray(triple(np.ascontiguousarray(table.T))),
    )
    hbm = pl.BlockSpec(memory_space=pltpu.HBM)
    shapes = (
        jax.ShapeDtypeStruct((samples, edges), F32),
        jax.ShapeDtypeStruct((1, elements), F32),
    )
    strip = pltpu.VMEM((samples, face), F32)
    slotted = pltpu.VMEM((GROUP, ring * CAP, GE), F32)
    adjoint, grad = pl.pallas_call(
        functools.partial(kernel, stators, axials),
        out_shape=shapes,
        in_specs=[hbm] * len(operands),
        out_specs=(hbm, hbm),
        scratch_shapes=[pltpu.VMEM(operand.shape, operand.dtype) for operand in operands]
        + [
            strip,
            strip,
            strip,
            pltpu.VMEM((CAP, rows), F32),
            pltpu.VMEM((GROUP, ring * CAP, rows), F32),
            pltpu.VMEM((GROUP, samples * QB, GE), F32),
            slotted,
            slotted,
            slotted,
            slotted,
            slotted,
            pltpu.VMEM((samples, edges + face), F32),
            pltpu.VMEM((6, samples, elements), F32),
            pltpu.VMEM((edges + face, 6 * CHUNK), BF16),
            pltpu.VMEM((edges + face, 2 * samples), F32),
            pltpu.VMEM((samples, edges), F32),
            pltpu.VMEM((1, elements), F32),
            pltpu.SemaphoreType.DMA((len(operands),)),
            pltpu.SemaphoreType.DMA((8,)),
            pltpu.SemaphoreType.DMA((8,)),
            pltpu.SemaphoreType.DMA((3,)),
        ],
        compiler_params=pltpu.CompilerParams(
            collective_id=0, has_side_effects=True, vmem_limit_bytes=56 * 1024 * 1024
        ),
    )(*operands)
    vmem = pl.BlockSpec(memory_space=pltpu.VMEM)
    adjoint, grad = pl.pallas_call(flush, out_shape=shapes, in_specs=[vmem, vmem], out_specs=(vmem, vmem))(adjoint, grad)
    return adjoint, grad.reshape(elements)


def solution(mesh):
    placed = (
        P(None, ("stator", "axial")),
        P(None, ("stator", "axial")),
        P(None, None, ("stator", "axial")),
        P(None, None, ("stator", "axial")),
        P(None, None, ("stator", "axial")),
        P(("stator", "axial")),
        P(),
        P(("stator", "axial"), None),
        P(("stator", "axial")),
    )
    return jax.shard_map(
        on_device,
        mesh=mesh,
        in_specs=placed,
        out_specs=(P(None, ("stator", "axial")), P(("stator", "axial"))),
        check_vma=False,
    )
```

```python
import functools
import math

import jax
import jax.numpy as jnp
import numpy as np
from jax import lax
from jax.experimental import pallas as pl
from jax.experimental.pallas import tpu as pltpu
from jax.sharding import PartitionSpec as P

GE = 128
GB = 4
QB = 2
CAP = 4
PENALTY = 4.0
SIMP_POWER = 3.0
CHUNK = 256
EARLY = 2
GROUP = 8

MESH = pl.DeviceIdType.MESH
F32 = jnp.float32
BF16 = jnp.bfloat16
NN = (((1,), (0,)), ((), ()))
NT = (((1,), (1,)), ((), ()))


def dft_table(count):
    rows = np.arange(count, dtype=np.float64)[:, None]
    index = np.arange(count)
    harmonic = ((index + 1) // 2).astype(np.float64)[None, :]
    is_sine = ((index % 2 == 0) & (index > 0))[None, :]
    angle = 2.0 * math.pi * harmonic * rows / count
    table = np.where(is_sine, np.sin(angle), np.cos(angle))
    return (table * math.sqrt(2.0 / count)).astype(np.float32)


def triple(table):
    high = table.astype(jnp.bfloat16)
    low = (table - high.astype(np.float32)).astype(jnp.bfloat16)
    return np.concatenate([high, high, low], 1)


def back_table(table):
    scaled = np.kron(np.eye(GB, dtype=np.float32), -PENALTY * table.T).astype(np.float32)
    high = scaled.astype(jnp.bfloat16)
    low = (scaled - high.astype(np.float32)).astype(jnp.bfloat16)
    return np.concatenate([high, low], 0)


def split(value):
    high = value.astype(BF16)
    return high, (value - high.astype(F32)).astype(BF16)


def mul(a, b, dims=NN):
    return lax.dot_general(a, b, dims, preferred_element_type=F32)


def table_dot(table, value):
    high, low = split(value)
    return mul(table, jnp.concatenate([high, low, high], 0))


def dot3(a, b, dims=NN):
    a_high, a_low = split(a)
    b_high, b_low = split(b)
    return mul(a_high, b_high, dims) + mul(a_high, b_low, dims) + mul(a_low, b_high, dims)


def side_by_side(value):
    return jnp.concatenate(split(value), 1)


def add_halves(value):
    half = value.shape[1] // 2
    return value[:, :half] + value[:, half:]


def as_bf16(mask):
    return jnp.where(mask, F32(1), F32(0)).astype(BF16)


def iota(shape, dim):
    return lax.broadcasted_iota(jnp.int32, shape, dim)


def kernel(
    stators,
    axials,
    coeffs_hbm,
    edge_hbm,
    curl_hbm,
    jac_hbm,
    fwd_hbm,
    density_hbm,
    mortar_hbm,
    peers_hbm,
    blocks_hbm,
    table_hbm,
    table_t_hbm,
    back_hbm,
    adjoint,
    grad,
    coeffs,
    edge,
    curl,
    jac,
    fwd,
    density,
    mortar,
    peers,
    blocks,
    table,
    table_t,
    back,
    upper,
    lower_out,
    lower_in,
    code_own,
    codes,
    mapped,
    rotor_out,
    rotor_mid,
    rotor_in,
    reply_out,
    reply_in,
    ext,
    values,
    acc,
    load,
    send,
    recv,
):
    samples, edges = coeffs.shape
    face = edges // 8
    extended = edges + face
    rows = samples * GB
    ring = stators // GROUP
    rotor_start = edges - GB * GE
    me, ax = lax.axis_index("stator"), lax.axis_index("axial")
    z, w = lax.div(me, GROUP), lax.rem(me, GROUP)
    above, below = lax.rem(ax + 1, axials), lax.rem(ax + axials - 1, axials)

    arrivals = []
    for index, (source, target) in enumerate(
        (
            (peers_hbm, peers),
            (blocks_hbm, blocks),
            (coeffs_hbm, coeffs),
            (table_hbm, table),
            (mortar_hbm, mortar),
            (edge_hbm, edge),
            (curl_hbm, curl),
            (jac_hbm, jac),
            (fwd_hbm, fwd),
            (density_hbm, density),
            (table_t_hbm, table_t),
            (back_hbm, back),
        )
    ):
        arrivals.append(pltpu.make_async_copy(source, target, load.at[index]))
        arrivals[-1].start()

    along_z = sorted(range(1, ring), key=lambda step: -min(step, ring - step))
    along_w = sorted(range(1, GROUP), key=lambda step: -min(step, GROUP - step))
    z_peers = [lax.rem(z + step, ring) for step in along_z]
    w_peers = [lax.rem(w + step, GROUP) for step in along_w]

    barrier = pltpu.get_barrier_semaphore()

    def greet(stator, axial):
        pl.semaphore_signal(barrier, inc=1, device_id=(stator, axial), device_id_type=MESH)

    for other in z_peers:
        greet(other * GROUP + w, ax)
    for other in w_peers:
        greet(z * GROUP + other, ax)
    for other in (above, below):
        greet(me, other)

    def push(source, target, index, stator, axial):
        copy = pltpu.make_async_remote_copy(
            src_ref=source,
            dst_ref=target,
            send_sem=send.at[index],
            recv_sem=recv.at[index],
            device_id=(stator, axial),
            device_id_type=MESH,
        )
        copy.start()
        return copy

    def await_bytes(view, sem):
        pltpu.make_async_copy(view, view, sem).wait()

    arrivals[0].wait()
    arrivals[1].wait()
    a, b = iota((rows, rows), 0), iota((rows, rows), 1)
    own_order = b == lax.rem(a, samples) * GB + lax.div(a, samples)
    listed = (peers[...] * QB + blocks[...]).astype(F32)
    col = jnp.sum(jnp.where(own_order, listed, 0.0), axis=1, keepdims=True)
    row = jnp.sum(jnp.where(a == b, col, 0.0), axis=0, keepdims=True)
    peer_col, peer_row = jnp.floor(col * 0.5), jnp.floor(row * 0.5)
    same = peer_col == peer_row
    rank_row = jnp.sum(jnp.where(same & (a < b), 1.0, 0.0), axis=0, keepdims=True)
    rank_col = jnp.sum(jnp.where(same & (b < a), 1.0, 0.0), axis=1, keepdims=True)

    def slot(peer, rank):
        ring_place = jnp.floor(peer * (1.0 / GROUP))
        group_place = peer - GROUP * ring_place
        return (group_place * (ring * CAP) + ring_place * CAP + rank).astype(jnp.int32)

    slot_row, slot_col = slot(peer_row, rank_row), slot(peer_col, rank_col)
    code_row = (peer_row * CAP + rank_row) * QB + (row - 2.0 * peer_row)
    code_own[...] = jnp.broadcast_to(code_row, (CAP, rows))

    arrivals[2].wait()
    arrivals[3].wait()
    arrivals[4].wait()
    own = table_dot(table[...], coeffs[...])
    ext[:, 0:edges] = own
    slots = stators * CAP
    rotor = jnp.concatenate(
        [own[:, rotor_start + b * GE : rotor_start + (b + 1) * GE] for b in range(GB)], 0
    )
    placed = as_bf16(iota((slots, rows), 0) == slot_row)
    rotor_out[...] = add_halves(mul(placed, side_by_side(rotor))).reshape(rotor_out.shape)
    faces = jnp.concatenate(
        [own[:, face + q * GE : face + (q + 1) * GE] for q in range(QB)], 0
    )
    own_mapped = dot3(faces, mortar[...])
    mapped[w] = own_mapped

    pl.semaphore_wait(barrier, (ring - 1) + (GROUP - 1) + 2)

    upper_copy = push(coeffs.at[:, pl.ds(0, face)], upper, 0, me, below)
    at_me = pl.ds(z * CAP, CAP)
    for other in z_peers:
        push(code_own, codes.at[w, at_me], 1, other * GROUP + w, ax)
    pltpu.make_async_copy(code_own, codes.at[w, at_me], recv.at[1]).start()
    for other in w_peers:
        push(mapped.at[w], mapped.at[w], 2, z * GROUP + other, ax)
    for other in z_peers:
        push(
            rotor_out.at[:, pl.ds(other * CAP, CAP)],
            rotor_mid.at[:, at_me],
            3,
            other * GROUP + w,
            ax,
        )
    pltpu.make_async_copy(rotor_out.at[:, at_me], rotor_mid.at[:, at_me], recv.at[3]).start()

    arrivals[5].wait()

    def pick(lanes, m):
        named = jnp.broadcast_to(edge[m : m + 1, lanes], (samples, GE))
        return named & (GE - 1), lax.shift_right_logical(named, GE.bit_length() - 1)

    def gather_own(part, carry):
        lanes = pl.ds(pl.multiple_of(part * GE, GE), GE)
        for m in range(6):
            low, high = pick(lanes, m)
            found = None
            for k in range(edges // GE):
                here = jnp.take_along_axis(ext[:, k * GE : (k + 1) * GE], low, axis=1)
                found = here if found is None else jnp.where(high == k, here, found)
            values[m, :, lanes] = found
        return carry

    lax.fori_loop(0, edges // GE, gather_own, 0)

    upper_copy.wait_recv()
    inside = jnp.where(ax < axials - 1, F32(1), F32(0))
    ext[:, edges:extended] = table_dot(table[...], upper[...] * inside)
    for index in range(6, 10):
        arrivals[index].wait()
    acc[...] = jnp.zeros_like(acc)

    def element_chunk(chunk, carry):
        lanes = pl.ds(pl.multiple_of(chunk * CHUNK, CHUNK), CHUNK)
        found = []
        for m in range(6):
            pieces = []
            for part in range(CHUNK // GE):
                here = pl.ds(pl.multiple_of(chunk * CHUNK + part * GE, GE), GE)
                low, high = pick(here, m)
                rim = jnp.take_along_axis(ext[:, edges:extended], low, axis=1)
                pieces.append(jnp.where(high == edges // GE, rim, values[m, :, here]))
            found.append(jnp.concatenate(pieces, 1))
        maps = curl[:, :, lanes]
        flux = [sum(maps[c, m : m + 1, :] * found[m] for m in range(6)) for c in range(3)]
        j = [jac[k, :, lanes].astype(F32) for k in range(6)]
        field = [
            j[0] * flux[0] + j[3] * flux[1] + j[4] * flux[2],
            j[3] * flux[0] + j[1] * flux[1] + j[5] * flux[2],
            j[4] * flux[0] + j[5] * flux[1] + j[2] * flux[2],
        ]
        energy = sum(flux[c] * fwd[c, :, lanes].astype(F32) for c in range(3))
        energy = jnp.sum(energy, axis=0, keepdims=True)
        dens = density[:, lanes]
        grad[:, lanes] = SIMP_POWER * dens * dens * energy / samples
        sub = iota((GE, CHUNK), 0).astype(jnp.int16)
        none = jnp.zeros((2 * samples, CHUNK), BF16)
        terms, hot = [], []
        for m in range(6):
            named = edge[m : m + 1, lanes]
            low = (named & (GE - 1)).astype(jnp.int16)
            high = lax.shift_right_logical(named, GE.bit_length() - 1)
            high = jnp.broadcast_to(high, (2 * samples, CHUNK)).astype(jnp.int16)
            hot.append(jnp.where(sub == low, BF16(1), BF16(0)))
            term = sum(maps[c, m : m + 1, :] * field[c] for c in range(3))
            term = jnp.concatenate(split(term), 0)
            terms.append(
                jnp.concatenate(
                    [jnp.where(high == jnp.int16(k), term, none) for k in range(extended // GE)], 0
                )
            )
        acc[...] += mul(jnp.concatenate(terms, 1), jnp.concatenate(hot, 1), NT)
        return carry

    chunks = edges // CHUNK
    lax.fori_loop(0, EARLY, element_chunk, 0)

    await_bytes(codes.at[w], recv.at[1])
    for other in w_peers:
        push(codes.at[w], codes.at[w], 5, z * GROUP + other, ax)
    await_bytes(mapped.at[pl.ds(0, GROUP - 1)], recv.at[2])
    asked = codes[w]
    rank = lax.rem(iota((ring * CAP, rows), 0), CAP)

    def by_row(value):
        return jnp.concatenate([value] * GB, 0)

    for other in range(GROUP):
        hits = [
            as_bf16(asked == (((z * GROUP + other) * CAP + rank) * QB + q).astype(F32))
            for q in range(QB)
        ]
        source = side_by_side(mapped[other])
        source = [by_row(source[q * samples : (q + 1) * samples]) for q in range(QB)]
        reply_out[other] = add_halves(
            mul(jnp.concatenate(hits, 1), jnp.concatenate(source, 0))
        )
    for other in z_peers:
        push(
            reply_out.at[:, pl.ds(other * CAP, CAP)],
            reply_in.at[:, at_me],
            6,
            other * GROUP + w,
            ax,
        )
    pltpu.make_async_copy(reply_out.at[:, at_me], reply_in.at[:, at_me], recv.at[6]).start()

    await_bytes(rotor_mid, recv.at[3])
    for other in w_peers:
        push(rotor_mid.at[other], rotor_in.at[w], 7, z * GROUP + other, ax)
    rotor_in[w] = rotor_mid[w]

    lax.fori_loop(EARLY, chunks, element_chunk, 0)
    sums = acc[...].reshape(extended // GE, 2, samples, GE)
    sums = sums[:, 0] + sums[:, 1]
    sums = jnp.concatenate([sums[k] for k in range(extended // GE)], 1)
    lower_out[...] = sums[:, edges:extended]
    lower_copy = push(lower_out, lower_in, 4, me, above)

    await_bytes(codes.at[pl.ds(0, GROUP - 1)], recv.at[5])
    listed_t = codes[...].reshape(slots, rows).T
    rank_t = lax.rem(iota((rows, slots), 1), CAP)
    takers, counts = [], []
    for q in range(QB):
        hit = listed_t == ((me * CAP + rank_t) * QB + q).astype(F32)
        hit = jnp.where(hit, F32(1), F32(0))
        folded = sum(hit[b * samples : (b + 1) * samples] for b in range(GB))
        takers.append(folded.astype(BF16))
        counts.append(jnp.sum(folded, axis=1, keepdims=True))
    takers, counts = jnp.concatenate(takers, 0), jnp.concatenate(counts, 0)
    await_bytes(rotor_in.at[pl.ds(0, GROUP - 1)], recv.at[7])
    arrived = add_halves(mul(takers, side_by_side(rotor_in[...].reshape(slots, GE))))
    stator_term = -PENALTY * dot3(arrived - counts * mapped[w], mortar[...], NT)

    arrivals[10].wait()
    lower_copy.wait_recv()
    linked = jnp.where(ax > 0, F32(1), F32(0))
    residual = [sums[:, 0:face] + lower_in[...] * linked]
    for q in range(QB):
        here = sums[:, face + q * GE : face + (q + 1) * GE]
        residual.append(here + stator_term[q * samples : (q + 1) * samples])
    residual.append(sums[:, face + QB * GE : rotor_start])
    adjoint[:, 0:rotor_start] = table_dot(table_t[...], jnp.concatenate(residual, 1))
    jumping = [
        sums[:, rotor_start + b * GE : rotor_start + (b + 1) * GE]
        + PENALTY * rotor[b * samples : (b + 1) * samples]
        for b in range(GB)
    ]
    base = table_dot(table_t[...], jnp.concatenate(jumping, 1))
    arrivals[11].wait()
    chosen = as_bf16(iota((rows, slots), 1) == slot_col)
    chosen = mul(back[...], chosen).astype(BF16)

    upper_copy.wait_send()
    lower_copy.wait_send()
    await_bytes(codes.at[0, pl.ds(0, (ring - 1) * CAP)], send.at[1])
    await_bytes(mapped.at[pl.ds(0, GROUP - 1)], send.at[2])
    await_bytes(rotor_mid.at[:, pl.ds(0, (ring - 1) * CAP)], send.at[3])
    await_bytes(codes.at[pl.ds(0, GROUP - 1)], send.at[5])
    await_bytes(rotor_in.at[pl.ds(0, GROUP - 1)], send.at[7])

    await_bytes(reply_in, recv.at[6])
    facing = mul(chosen, side_by_side(reply_in[...].reshape(slots, GE)))
    facing = add_halves(facing[:rows]) + facing[rows:, :GE]
    for b in range(GB):
        lanes = slice(rotor_start + b * GE, rotor_start + (b + 1) * GE)
        adjoint[:, lanes] = (
            base[:, b * GE : (b + 1) * GE] + facing[b * samples : (b + 1) * samples]
        )
    await_bytes(reply_out.at[:, pl.ds(0, (ring - 1) * CAP)], send.at[6])


def flush(adjoint, grad, adjoint_hbm, grad_hbm, sems):
    copies = (
        pltpu.make_async_copy(adjoint, adjoint_hbm, sems.at[0]),
        pltpu.make_async_copy(grad, grad_hbm, sems.at[1]),
    )
    for copy in copies:
        copy.start()
    for copy in copies:
        copy.wait()


def on_device(coeffs, elem_edge, curl_map, jacobian, flux_fwd, density, mortar, gap_peer, gap_block):
    stators, axials = lax.axis_size("stator"), lax.axis_size("axial")
    samples, edges = coeffs.shape
    elements = elem_edge.shape[1]
    face = edges // 8
    rows = samples * GB
    ring = stators // GROUP
    table = dft_table(samples)
    operands = (
        coeffs,
        elem_edge,
        curl_map,
        jacobian,
        flux_fwd,
        density.reshape(1, elements),
        mortar,
        gap_peer.reshape(1, rows),
        gap_block.reshape(1, rows),
        jnp.asarray(triple(table)),
        jnp.asarray(triple(np.ascontiguousarray(table.T))),
        jnp.asarray(back_table(table)),
    )
    vmem = pl.BlockSpec(memory_space=pltpu.VMEM)
    hbm = pl.BlockSpec(memory_space=pltpu.HBM)
    shapes = (
        jax.ShapeDtypeStruct((samples, edges), F32),
        jax.ShapeDtypeStruct((1, elements), F32),
    )
    strip = pltpu.VMEM((samples, face), F32)
    slotted = pltpu.VMEM((GROUP, ring * CAP, GE), F32)
    results = pl.pallas_call(
        functools.partial(kernel, stators, axials),
        out_shape=shapes,
        in_specs=[hbm] * len(operands),
        out_specs=(vmem, vmem),
        scratch_shapes=[pltpu.VMEM(operand.shape, operand.dtype) for operand in operands]
        + [
            strip,
            strip,
            strip,
            pltpu.VMEM((CAP, rows), F32),
            pltpu.VMEM((GROUP, ring * CAP, rows), F32),
            pltpu.VMEM((GROUP, samples * QB, GE), F32),
            slotted,
            slotted,
            slotted,
            slotted,
            slotted,
            pltpu.VMEM((samples, edges + face), F32),
            pltpu.VMEM((6, samples, elements), F32),
            pltpu.VMEM(((edges + face) // GE * 2 * samples, GE), F32),
            pltpu.SemaphoreType.DMA((len(operands),)),
            pltpu.SemaphoreType.DMA((8,)),
            pltpu.SemaphoreType.DMA((8,)),
        ],
        compiler_params=pltpu.CompilerParams(
            collective_id=0, has_side_effects=True, vmem_limit_bytes=32 * 1024 * 1024
        ),
    )(*(pltpu.with_memory_space_constraint(operand, pltpu.HBM) for operand in operands))
    adjoint, grad = pl.pallas_call(
        flush,
        out_shape=shapes,
        in_specs=[vmem, vmem],
        out_specs=(hbm, hbm),
        scratch_shapes=[pltpu.SemaphoreType.DMA((2,))],
    )(*(pltpu.with_memory_space_constraint(result, pltpu.VMEM) for result in results))
    return adjoint, grad.reshape(elements)


def solution(mesh):
    placed = (
        P(None, ("stator", "axial")),
        P(None, ("stator", "axial")),
        P(None, None, ("stator", "axial")),
        P(None, None, ("stator", "axial")),
        P(None, None, ("stator", "axial")),
        P(("stator", "axial")),
        P(),
        P(("stator", "axial"), None),
        P(("stator", "axial")),
    )
    return jax.shard_map(
        on_device,
        mesh=mesh,
        in_specs=placed,
        out_specs=(P(None, ("stator", "axial")), P(("stator", "axial"))),
        check_vma=False,
    )
```

```python
import functools
import math

import jax
import jax.numpy as jnp
import numpy as np
from jax import lax
from jax.experimental import pallas as pl
from jax.experimental.pallas import tpu as pltpu
from jax.sharding import PartitionSpec as P

GE = 128
GB = 4
QB = 2
CAP = 4
PENALTY = 4.0
SIMP_POWER = 3.0
CHUNK = 256
EARLY = 2
GROUP = 8

MESH = pl.DeviceIdType.MESH
F32 = jnp.float32
BF16 = jnp.bfloat16
NN = (((1,), (0,)), ((), ()))
NT = (((1,), (1,)), ((), ()))


def dft_table(count):
    rows = np.arange(count, dtype=np.float64)[:, None]
    index = np.arange(count)
    harmonic = ((index + 1) // 2).astype(np.float64)[None, :]
    is_sine = ((index % 2 == 0) & (index > 0))[None, :]
    angle = 2.0 * math.pi * harmonic * rows / count
    table = np.where(is_sine, np.sin(angle), np.cos(angle))
    return (table * math.sqrt(2.0 / count)).astype(np.float32)


def triple(table):
    high = table.astype(jnp.bfloat16)
    low = (table - high.astype(np.float32)).astype(jnp.bfloat16)
    return np.concatenate([high, high, low], 1)


def back_table(table):
    scaled = np.kron(np.eye(GB, dtype=np.float32), -PENALTY * table.T).astype(np.float32)
    high = scaled.astype(jnp.bfloat16)
    low = (scaled - high.astype(np.float32)).astype(jnp.bfloat16)
    return np.concatenate([high, low], 0)


def split(value):
    high = value.astype(BF16)
    return high, (value - high.astype(F32)).astype(BF16)


def mul(a, b, dims=NN):
    return lax.dot_general(a, b, dims, preferred_element_type=F32)


def table_dot(table, value):
    high, low = split(value)
    return mul(table, jnp.concatenate([high, low, high], 0))


def dot3(a, b, dims=NN):
    a_high, a_low = split(a)
    b_high, b_low = split(b)
    return mul(a_high, b_high, dims) + mul(a_high, b_low, dims) + mul(a_low, b_high, dims)


def side_by_side(value):
    return jnp.concatenate(split(value), 1)


def add_halves(value):
    half = value.shape[1] // 2
    return value[:, :half] + value[:, half:]


def as_bf16(mask):
    return jnp.where(mask, F32(1), F32(0)).astype(BF16)


def iota(shape, dim):
    return lax.broadcasted_iota(jnp.int32, shape, dim)


def kernel(
    stators,
    axials,
    coeffs_hbm,
    edge_hbm,
    curl_hbm,
    jac_hbm,
    fwd_hbm,
    density_hbm,
    mortar_hbm,
    peers_hbm,
    blocks_hbm,
    table_hbm,
    table_t_hbm,
    back_hbm,
    adjoint,
    grad,
    coeffs,
    edge,
    curl,
    jac,
    fwd,
    density,
    mortar,
    peers,
    blocks,
    table,
    table_t,
    back,
    upper,
    lower_out,
    lower_in,
    code_own,
    codes,
    mapped,
    rotor_out,
    rotor_mid,
    rotor_in,
    reply_out,
    reply_in,
    ext,
    values,
    acc,
    load,
    send,
    recv,
):
    samples, edges = coeffs.shape
    face = edges // 8
    extended = edges + face
    rows = samples * GB
    ring = stators // GROUP
    rotor_start = edges - GB * GE
    me, ax = lax.axis_index("stator"), lax.axis_index("axial")
    z, w = lax.div(me, GROUP), lax.rem(me, GROUP)
    above, below = lax.rem(ax + 1, axials), lax.rem(ax + axials - 1, axials)

    along_z = sorted(range(1, ring), key=lambda step: -min(step, ring - step))
    along_w = sorted(range(1, GROUP), key=lambda step: -min(step, GROUP - step))
    z_peers = [lax.rem(z + step, ring) for step in along_z]
    w_peers = [lax.rem(w + step, GROUP) for step in along_w]

    barrier = pltpu.get_barrier_semaphore()

    def greet(stator, axial):
        pl.semaphore_signal(barrier, inc=1, device_id=(stator, axial), device_id_type=MESH)

    for other in z_peers:
        greet(other * GROUP + w, ax)
    for other in w_peers:
        greet(z * GROUP + other, ax)
    for other in (above, below):
        greet(me, other)

    arrivals = []
    for index, (source, target) in enumerate(
        (
            (peers_hbm, peers),
            (blocks_hbm, blocks),
            (coeffs_hbm, coeffs),
            (table_hbm, table),
            (mortar_hbm, mortar),
            (edge_hbm, edge),
            (curl_hbm, curl),
            (jac_hbm, jac),
            (fwd_hbm, fwd),
            (density_hbm, density),
            (table_t_hbm, table_t),
            (back_hbm, back),
        )
    ):
        arrivals.append(pltpu.make_async_copy(source, target, load.at[index]))
        arrivals[-1].start()

    def push(source, target, index, stator, axial):
        copy = pltpu.make_async_remote_copy(
            src_ref=source,
            dst_ref=target,
            send_sem=send.at[index],
            recv_sem=recv.at[index],
            device_id=(stator, axial),
            device_id_type=MESH,
        )
        copy.start()
        return copy

    def await_bytes(view, sem):
        pltpu.make_async_copy(view, view, sem).wait()

    arrivals[2].wait()
    arrivals[3].wait()
    arrivals[4].wait()
    own = table_dot(table[...], coeffs[...])
    ext[:, 0:edges] = own
    faces = jnp.concatenate(
        [own[:, face + q * GE : face + (q + 1) * GE] for q in range(QB)], 0
    )
    own_mapped = dot3(faces, mortar[...])
    mapped[w] = own_mapped

    arrivals[0].wait()
    arrivals[1].wait()
    a, b = iota((rows, rows), 0), iota((rows, rows), 1)
    own_order = b == lax.rem(a, samples) * GB + lax.div(a, samples)
    listed = (peers[...] * QB + blocks[...]).astype(F32)
    col = jnp.sum(jnp.where(own_order, listed, 0.0), axis=1, keepdims=True)
    row = jnp.sum(jnp.where(a == b, col, 0.0), axis=0, keepdims=True)
    peer_col, peer_row = jnp.floor(col * 0.5), jnp.floor(row * 0.5)
    same = peer_col == peer_row
    rank_row = jnp.sum(jnp.where(same & (a < b), 1.0, 0.0), axis=0, keepdims=True)
    rank_col = jnp.sum(jnp.where(same & (b < a), 1.0, 0.0), axis=1, keepdims=True)

    def slot(peer, rank):
        ring_place = jnp.floor(peer * (1.0 / GROUP))
        group_place = peer - GROUP * ring_place
        return (group_place * (ring * CAP) + ring_place * CAP + rank).astype(jnp.int32)

    slot_row, slot_col = slot(peer_row, rank_row), slot(peer_col, rank_col)
    code_row = (peer_row * CAP + rank_row) * QB + (row - 2.0 * peer_row)
    code_own[...] = jnp.broadcast_to(code_row, (CAP, rows))

    slots = stators * CAP
    rotor = jnp.concatenate(
        [own[:, rotor_start + b * GE : rotor_start + (b + 1) * GE] for b in range(GB)], 0
    )
    placed = as_bf16(iota((slots, rows), 0) == slot_row)
    rotor_out[...] = add_halves(mul(placed, side_by_side(rotor))).reshape(rotor_out.shape)
    pl.semaphore_wait(barrier, (ring - 1) + (GROUP - 1) + 2)

    at_me = pl.ds(z * CAP, CAP)
    for other in z_peers:
        push(code_own, codes.at[w, at_me], 1, other * GROUP + w, ax)
    pltpu.make_async_copy(code_own, codes.at[w, at_me], recv.at[1]).start()
    upper_copy = push(coeffs.at[:, pl.ds(0, face)], upper, 0, me, below)
    for other in w_peers:
        push(mapped.at[w], mapped.at[w], 2, z * GROUP + other, ax)
    for other in z_peers:
        push(
            rotor_out.at[:, pl.ds(other * CAP, CAP)],
            rotor_mid.at[:, at_me],
            3,
            other * GROUP + w,
            ax,
        )
    pltpu.make_async_copy(rotor_out.at[:, at_me], rotor_mid.at[:, at_me], recv.at[3]).start()

    arrivals[5].wait()

    def pick(lanes, m):
        named = jnp.broadcast_to(edge[m : m + 1, lanes], (samples, GE))
        return named & (GE - 1), lax.shift_right_logical(named, GE.bit_length() - 1)

    def gather_own(part, carry):
        lanes = pl.ds(pl.multiple_of(part * GE, GE), GE)
        for m in range(6):
            low, high = pick(lanes, m)
            found = None
            for k in range(edges // GE):
                here = jnp.take_along_axis(ext[:, k * GE : (k + 1) * GE], low, axis=1)
                found = here if found is None else jnp.where(high == k, here, found)
            values[m, :, lanes] = found
        return carry

    lax.fori_loop(0, edges // GE, gather_own, 0)

    upper_copy.wait_recv()
    inside = jnp.where(ax < axials - 1, F32(1), F32(0))
    ext[:, edges:extended] = table_dot(table[...], upper[...] * inside)
    for index in range(6, 10):
        arrivals[index].wait()
    acc[...] = jnp.zeros_like(acc)

    def element_chunk(chunk, carry):
        lanes = pl.ds(pl.multiple_of(chunk * CHUNK, CHUNK), CHUNK)
        found = []
        for m in range(6):
            pieces = []
            for part in range(CHUNK // GE):
                here = pl.ds(pl.multiple_of(chunk * CHUNK + part * GE, GE), GE)
                low, high = pick(here, m)
                rim = jnp.take_along_axis(ext[:, edges:extended], low, axis=1)
                pieces.append(jnp.where(high == edges // GE, rim, values[m, :, here]))
            found.append(jnp.concatenate(pieces, 1))
        maps = curl[:, :, lanes]
        flux = [sum(maps[c, m : m + 1, :] * found[m] for m in range(6)) for c in range(3)]
        j = [jac[k, :, lanes].astype(F32) for k in range(6)]
        field = [
            j[0] * flux[0] + j[3] * flux[1] + j[4] * flux[2],
            j[3] * flux[0] + j[1] * flux[1] + j[5] * flux[2],
            j[4] * flux[0] + j[5] * flux[1] + j[2] * flux[2],
        ]
        energy = sum(flux[c] * fwd[c, :, lanes].astype(F32) for c in range(3))
        energy = jnp.sum(energy, axis=0, keepdims=True)
        dens = density[:, lanes]
        grad[:, lanes] = SIMP_POWER * dens * dens * energy / samples
        sub = iota((GE, CHUNK), 0).astype(jnp.int16)
        none = jnp.zeros((2 * samples, CHUNK), BF16)
        terms, hot = [], []
        for m in range(6):
            named = edge[m : m + 1, lanes]
            low = (named & (GE - 1)).astype(jnp.int16)
            high = lax.shift_right_logical(named, GE.bit_length() - 1)
            high = jnp.broadcast_to(high, (2 * samples, CHUNK)).astype(jnp.int16)
            hot.append(jnp.where(sub == low, BF16(1), BF16(0)))
            term = sum(maps[c, m : m + 1, :] * field[c] for c in range(3))
            term = jnp.concatenate(split(term), 0)
            terms.append(
                jnp.concatenate(
                    [jnp.where(high == jnp.int16(k), term, none) for k in range(extended // GE)], 0
                )
            )
        acc[...] += mul(jnp.concatenate(terms, 1), jnp.concatenate(hot, 1), NT)
        return carry

    chunks = edges // CHUNK
    lax.fori_loop(0, EARLY, element_chunk, 0)

    await_bytes(codes.at[w], recv.at[1])
    for other in w_peers:
        push(codes.at[w], codes.at[w], 5, z * GROUP + other, ax)
    await_bytes(mapped.at[pl.ds(0, GROUP - 1)], recv.at[2])
    asked = codes[w]
    rank = lax.rem(iota((ring * CAP, rows), 0), CAP)

    def by_row(value):
        return jnp.concatenate([value] * GB, 0)

    for other in range(GROUP):
        hits = [
            as_bf16(asked == (((z * GROUP + other) * CAP + rank) * QB + q).astype(F32))
            for q in range(QB)
        ]
        source = side_by_side(mapped[other])
        source = [by_row(source[q * samples : (q + 1) * samples]) for q in range(QB)]
        reply_out[other] = add_halves(
            mul(jnp.concatenate(hits, 1), jnp.concatenate(source, 0))
        )
    for other in z_peers:
        push(
            reply_out.at[:, pl.ds(other * CAP, CAP)],
            reply_in.at[:, at_me],
            6,
            other * GROUP + w,
            ax,
        )
    pltpu.make_async_copy(reply_out.at[:, at_me], reply_in.at[:, at_me], recv.at[6]).start()

    await_bytes(rotor_mid, recv.at[3])
    for other in w_peers:
        push(rotor_mid.at[other], rotor_in.at[w], 7, z * GROUP + other, ax)
    rotor_in[w] = rotor_mid[w]

    lax.fori_loop(EARLY, chunks, element_chunk, 0)
    sums = acc[...].reshape(extended // GE, 2, samples, GE)
    sums = sums[:, 0] + sums[:, 1]
    sums = jnp.concatenate([sums[k] for k in range(extended // GE)], 1)
    lower_out[...] = sums[:, edges:extended]
    lower_copy = push(lower_out, lower_in, 4, me, above)

    local = jnp.concatenate(
        [sums[:, 0:rotor_start]]
        + [
            sums[:, rotor_start + b * GE : rotor_start + (b + 1) * GE]
            + PENALTY * rotor[b * samples : (b + 1) * samples]
            for b in range(GB)
        ],
        1,
    )
    arrivals[10].wait()
    adjoint[...] = table_dot(table_t[...], local)
    arrivals[11].wait()
    chosen = as_bf16(iota((rows, slots), 1) == slot_col)
    chosen = mul(back[...], chosen).astype(BF16)

    await_bytes(codes.at[pl.ds(0, GROUP - 1)], recv.at[5])
    listed_t = codes[...].reshape(slots, rows).T
    rank_t = lax.rem(iota((rows, slots), 1), CAP)
    takers, counts = [], []
    for q in range(QB):
        hit = listed_t == ((me * CAP + rank_t) * QB + q).astype(F32)
        hit = jnp.where(hit, F32(1), F32(0))
        folded = sum(hit[b * samples : (b + 1) * samples] for b in range(GB))
        takers.append(folded.astype(BF16))
        counts.append(jnp.sum(folded, axis=1, keepdims=True))
    takers, counts = jnp.concatenate(takers, 0), jnp.concatenate(counts, 0)
    counted = counts * mapped[w]
    await_bytes(rotor_in.at[pl.ds(0, GROUP - 1)], recv.at[7])
    arrived = add_halves(mul(takers, side_by_side(rotor_in[...].reshape(slots, GE))))
    stator_term = -PENALTY * dot3(arrived - counted, mortar[...], NT)
    stator_term = jnp.concatenate(
        [stator_term[q * samples : (q + 1) * samples] for q in range(QB)], 1
    )
    adjoint[:, face : face + QB * GE] += table_dot(table_t[...], stator_term)

    lower_copy.wait_recv()
    linked = jnp.where(ax > 0, F32(1), F32(0))
    adjoint[:, 0:face] += table_dot(table_t[...], lower_in[...] * linked)

    await_bytes(reply_in, recv.at[6])
    facing = mul(chosen, side_by_side(reply_in[...].reshape(slots, GE)))
    facing = add_halves(facing[:rows]) + facing[rows:, :GE]
    for b in range(GB):
        lanes = slice(rotor_start + b * GE, rotor_start + (b + 1) * GE)
        adjoint[:, lanes] += facing[b * samples : (b + 1) * samples]

    upper_copy.wait_send()
    lower_copy.wait_send()
    await_bytes(codes.at[0, pl.ds(0, (ring - 1) * CAP)], send.at[1])
    await_bytes(mapped.at[pl.ds(0, GROUP - 1)], send.at[2])
    await_bytes(rotor_mid.at[:, pl.ds(0, (ring - 1) * CAP)], send.at[3])
    await_bytes(codes.at[pl.ds(0, GROUP - 1)], send.at[5])
    await_bytes(reply_out.at[:, pl.ds(0, (ring - 1) * CAP)], send.at[6])
    await_bytes(rotor_in.at[pl.ds(0, GROUP - 1)], send.at[7])


def flush(adjoint, grad, adjoint_hbm, grad_hbm, sems):
    copies = (
        pltpu.make_async_copy(adjoint, adjoint_hbm, sems.at[0]),
        pltpu.make_async_copy(grad, grad_hbm, sems.at[1]),
    )
    for copy in copies:
        copy.start()
    for copy in copies:
        copy.wait()


def on_device(coeffs, elem_edge, curl_map, jacobian, flux_fwd, density, mortar, gap_peer, gap_block):
    stators, axials = lax.axis_size("stator"), lax.axis_size("axial")
    samples, edges = coeffs.shape
    elements = elem_edge.shape[1]
    face = edges // 8
    rows = samples * GB
    ring = stators // GROUP
    table = dft_table(samples)
    operands = (
        coeffs,
        elem_edge,
        curl_map,
        jacobian,
        flux_fwd,
        density.reshape(1, elements),
        mortar,
        gap_peer.reshape(1, rows),
        gap_block.reshape(1, rows),
        jnp.asarray(triple(table)),
        jnp.asarray(triple(np.ascontiguousarray(table.T))),
        jnp.asarray(back_table(table)),
    )
    vmem = pl.BlockSpec(memory_space=pltpu.VMEM)
    hbm = pl.BlockSpec(memory_space=pltpu.HBM)
    shapes = (
        jax.ShapeDtypeStruct((samples, edges), F32),
        jax.ShapeDtypeStruct((1, elements), F32),
    )
    strip = pltpu.VMEM((samples, face), F32)
    slotted = pltpu.VMEM((GROUP, ring * CAP, GE), F32)
    results = pl.pallas_call(
        functools.partial(kernel, stators, axials),
        out_shape=shapes,
        in_specs=[hbm] * len(operands),
        out_specs=(vmem, vmem),
        scratch_shapes=[pltpu.VMEM(operand.shape, operand.dtype) for operand in operands]
        + [
            strip,
            strip,
            strip,
            pltpu.VMEM((CAP, rows), F32),
            pltpu.VMEM((GROUP, ring * CAP, rows), F32),
            pltpu.VMEM((GROUP, samples * QB, GE), F32),
            slotted,
            slotted,
            slotted,
            slotted,
            slotted,
            pltpu.VMEM((samples, edges + face), F32),
            pltpu.VMEM((6, samples, elements), F32),
            pltpu.VMEM(((edges + face) // GE * 2 * samples, GE), F32),
            pltpu.SemaphoreType.DMA((len(operands),)),
            pltpu.SemaphoreType.DMA((8,)),
            pltpu.SemaphoreType.DMA((8,)),
        ],
        compiler_params=pltpu.CompilerParams(
            collective_id=0, has_side_effects=True, vmem_limit_bytes=32 * 1024 * 1024
        ),
    )(*(pltpu.with_memory_space_constraint(operand, pltpu.HBM) for operand in operands))
    adjoint, grad = pl.pallas_call(
        flush,
        out_shape=shapes,
        in_specs=[vmem, vmem],
        out_specs=(hbm, hbm),
        scratch_shapes=[pltpu.SemaphoreType.DMA((2,))],
    )(*(pltpu.with_memory_space_constraint(result, pltpu.VMEM) for result in results))
    return adjoint, grad.reshape(elements)


def solution(mesh):
    placed = (
        P(None, ("stator", "axial")),
        P(None, ("stator", "axial")),
        P(None, None, ("stator", "axial")),
        P(None, None, ("stator", "axial")),
        P(None, None, ("stator", "axial")),
        P(("stator", "axial")),
        P(),
        P(("stator", "axial"), None),
        P(("stator", "axial")),
    )
    return jax.shard_map(
        on_device,
        mesh=mesh,
        in_specs=placed,
        out_specs=(P(None, ("stator", "axial")), P(("stator", "axial"))),
        check_vma=False,
    )
```

```python
import functools
import math

import jax
import jax.numpy as jnp
import numpy as np
from jax import lax
from jax.experimental import pallas as pl
from jax.experimental.pallas import tpu as pltpu
from jax.sharding import PartitionSpec as P

GE = 128
GB = 4
QB = 2
CAP = 4
PENALTY = 4.0
SIMP_POWER = 3.0
CHUNK = 256
EARLY = 2
GROUP = 8

MESH = pl.DeviceIdType.MESH
F32 = jnp.float32
BF16 = jnp.bfloat16
NN = (((1,), (0,)), ((), ()))
NT = (((1,), (1,)), ((), ()))


def dft_table(count):
    rows = np.arange(count, dtype=np.float64)[:, None]
    index = np.arange(count)
    harmonic = ((index + 1) // 2).astype(np.float64)[None, :]
    is_sine = ((index % 2 == 0) & (index > 0))[None, :]
    angle = 2.0 * math.pi * harmonic * rows / count
    table = np.where(is_sine, np.sin(angle), np.cos(angle))
    return (table * math.sqrt(2.0 / count)).astype(np.float32)


def triple(table):
    high = table.astype(jnp.bfloat16)
    low = (table - high.astype(np.float32)).astype(jnp.bfloat16)
    return np.concatenate([high, high, low], 1)


def back_table(table):
    scaled = np.kron(np.eye(GB, dtype=np.float32), -PENALTY * table.T).astype(np.float32)
    high = scaled.astype(jnp.bfloat16)
    low = (scaled - high.astype(np.float32)).astype(jnp.bfloat16)
    return np.concatenate([high, low], 0)


def split(value):
    high = value.astype(BF16)
    return high, (value - high.astype(F32)).astype(BF16)


def mul(a, b, dims=NN):
    return lax.dot_general(a, b, dims, preferred_element_type=F32)


def table_dot(table, value):
    high, low = split(value)
    return mul(table, jnp.concatenate([high, low, high], 0))


def dot3(a, b, dims=NN):
    a_high, a_low = split(a)
    b_high, b_low = split(b)
    return mul(a_high, b_high, dims) + mul(a_high, b_low, dims) + mul(a_low, b_high, dims)


def side_by_side(value):
    return jnp.concatenate(split(value), 1)


def add_halves(value):
    half = value.shape[1] // 2
    return value[:, :half] + value[:, half:]


def as_bf16(mask):
    return jnp.where(mask, F32(1), F32(0)).astype(BF16)


def iota(shape, dim):
    return lax.broadcasted_iota(jnp.int32, shape, dim)


def kernel(
    stators,
    axials,
    coeffs_hbm,
    edge_hbm,
    curl_hbm,
    jac_hbm,
    fwd_hbm,
    density_hbm,
    mortar_hbm,
    peers_hbm,
    blocks_hbm,
    table_hbm,
    table_t_hbm,
    back_hbm,
    adjoint,
    grad,
    coeffs,
    edge,
    curl,
    jac,
    fwd,
    density,
    mortar,
    peers,
    blocks,
    table,
    table_t,
    back,
    upper,
    lower_out,
    lower_in,
    code_own,
    codes,
    mapped,
    rotor_out,
    rotor_mid,
    rotor_in,
    reply_out,
    reply_in,
    ext,
    values,
    acc,
    load,
    send,
    recv,
):
    samples, edges = coeffs.shape
    face = edges // 8
    extended = edges + face
    rows = samples * GB
    ring = stators // GROUP
    rotor_start = edges - GB * GE
    me, ax = lax.axis_index("stator"), lax.axis_index("axial")
    z, w = lax.div(me, GROUP), lax.rem(me, GROUP)
    above, below = lax.rem(ax + 1, axials), lax.rem(ax + axials - 1, axials)

    along_z = sorted(range(1, ring), key=lambda step: -min(step, ring - step))
    along_w = sorted(range(1, GROUP), key=lambda step: -min(step, GROUP - step))
    z_peers = [lax.rem(z + step, ring) for step in along_z]
    w_peers = [lax.rem(w + step, GROUP) for step in along_w]

    barrier = pltpu.get_barrier_semaphore()

    def greet(stator, axial):
        pl.semaphore_signal(barrier, inc=1, device_id=(stator, axial), device_id_type=MESH)

    for other in z_peers:
        greet(other * GROUP + w, ax)
    for other in w_peers:
        greet(z * GROUP + other, ax)
    has_above, has_below = ax < axials - 1, ax > 0

    @pl.when(has_above)
    def _():
        greet(me, above)

    @pl.when(has_below)
    def _():
        greet(me, below)


    arrivals = []
    for index, (source, target) in enumerate(
        (
            (peers_hbm, peers),
            (blocks_hbm, blocks),
            (coeffs_hbm, coeffs),
            (table_hbm, table),
            (mortar_hbm, mortar),
            (edge_hbm, edge),
            (curl_hbm, curl),
            (jac_hbm, jac),
            (fwd_hbm, fwd),
            (density_hbm, density),
            (table_t_hbm, table_t),
            (back_hbm, back),
        )
    ):
        arrivals.append(pltpu.make_async_copy(source, target, load.at[index]))
        arrivals[-1].start()

    def transfer(source, target, index, stator, axial):
        return pltpu.make_async_remote_copy(
            src_ref=source,
            dst_ref=target,
            send_sem=send.at[index],
            recv_sem=recv.at[index],
            device_id=(stator, axial),
            device_id_type=MESH,
        )

    def push(*where):
        transfer(*where).start()

    def await_bytes(view, sem):
        pltpu.make_async_copy(view, view, sem).wait()

    arrivals[2].wait()
    arrivals[3].wait()
    arrivals[4].wait()
    own = table_dot(table[...], coeffs[...])
    ext[:, 0:edges] = own
    faces = jnp.concatenate(
        [own[:, face + q * GE : face + (q + 1) * GE] for q in range(QB)], 0
    )
    own_mapped = dot3(faces, mortar[...])
    mapped[w] = own_mapped

    arrivals[0].wait()
    arrivals[1].wait()
    a, b = iota((rows, rows), 0), iota((rows, rows), 1)
    own_order = b == lax.rem(a, samples) * GB + lax.div(a, samples)
    listed = (peers[...] * QB + blocks[...]).astype(F32)
    col = jnp.sum(jnp.where(own_order, listed, 0.0), axis=1, keepdims=True)
    row = jnp.sum(jnp.where(a == b, col, 0.0), axis=0, keepdims=True)
    peer_col, peer_row = jnp.floor(col * 0.5), jnp.floor(row * 0.5)
    same = peer_col == peer_row
    rank_row = jnp.sum(jnp.where(same & (a < b), 1.0, 0.0), axis=0, keepdims=True)
    rank_col = jnp.sum(jnp.where(same & (b < a), 1.0, 0.0), axis=1, keepdims=True)

    def slot(peer, rank):
        ring_place = jnp.floor(peer * (1.0 / GROUP))
        group_place = peer - GROUP * ring_place
        return (group_place * (ring * CAP) + ring_place * CAP + rank).astype(jnp.int32)

    slot_row, slot_col = slot(peer_row, rank_row), slot(peer_col, rank_col)
    code_row = (peer_row * CAP + rank_row) * QB + (row - 2.0 * peer_row)
    code_own[...] = jnp.broadcast_to(code_row, (CAP, rows))

    slots = stators * CAP
    rotor = jnp.concatenate(
        [own[:, rotor_start + b * GE : rotor_start + (b + 1) * GE] for b in range(GB)], 0
    )
    placed = as_bf16(iota((slots, rows), 0) == slot_row)
    rotor_out[...] = add_halves(mul(placed, side_by_side(rotor))).reshape(rotor_out.shape)
    neighbours = jnp.where(has_above, 1, 0) + jnp.where(has_below, 1, 0)
    pl.semaphore_wait(barrier, (ring - 1) + (GROUP - 1) + neighbours)

    at_me = pl.ds(z * CAP, CAP)
    for other in z_peers:
        push(code_own, codes.at[w, at_me], 1, other * GROUP + w, ax)
    pltpu.make_async_copy(code_own, codes.at[w, at_me], recv.at[1]).start()
    upper_copy = transfer(coeffs.at[:, pl.ds(0, face)], upper, 0, me, below)

    @pl.when(has_below)
    def _():
        upper_copy.start()

    for other in w_peers:
        push(mapped.at[w], mapped.at[w], 2, z * GROUP + other, ax)
    for other in z_peers:
        push(
            rotor_out.at[:, pl.ds(other * CAP, CAP)],
            rotor_mid.at[:, at_me],
            3,
            other * GROUP + w,
            ax,
        )
    pltpu.make_async_copy(rotor_out.at[:, at_me], rotor_mid.at[:, at_me], recv.at[3]).start()

    arrivals[5].wait()

    def pick(lanes, m):
        named = jnp.broadcast_to(edge[m : m + 1, lanes], (samples, GE))
        return named & (GE - 1), lax.shift_right_logical(named, GE.bit_length() - 1)

    def gather_own(part, carry):
        lanes = pl.ds(pl.multiple_of(part * GE, GE), GE)
        for m in range(6):
            low, high = pick(lanes, m)
            found = None
            for k in range(edges // GE):
                here = jnp.take_along_axis(ext[:, k * GE : (k + 1) * GE], low, axis=1)
                found = here if found is None else jnp.where(high == k, here, found)
            values[m, :, lanes] = found
        return carry

    lax.fori_loop(0, edges // GE, gather_own, 0)

    @pl.when(has_above)
    def _():
        upper_copy.wait_recv()

    @pl.when(jnp.logical_not(has_above))
    def _():
        upper[...] = jnp.zeros_like(upper)

    ext[:, edges:extended] = table_dot(table[...], upper[...])
    for index in range(6, 10):
        arrivals[index].wait()
    acc[...] = jnp.zeros_like(acc)

    def element_chunk(chunk, carry):
        lanes = pl.ds(pl.multiple_of(chunk * CHUNK, CHUNK), CHUNK)
        found = []
        for m in range(6):
            pieces = []
            for part in range(CHUNK // GE):
                here = pl.ds(pl.multiple_of(chunk * CHUNK + part * GE, GE), GE)
                low, high = pick(here, m)
                rim = jnp.take_along_axis(ext[:, edges:extended], low, axis=1)
                pieces.append(jnp.where(high == edges // GE, rim, values[m, :, here]))
            found.append(jnp.concatenate(pieces, 1))
        maps = curl[:, :, lanes]
        flux = [sum(maps[c, m : m + 1, :] * found[m] for m in range(6)) for c in range(3)]
        j = [jac[k, :, lanes].astype(F32) for k in range(6)]
        field = [
            j[0] * flux[0] + j[3] * flux[1] + j[4] * flux[2],
            j[3] * flux[0] + j[1] * flux[1] + j[5] * flux[2],
            j[4] * flux[0] + j[5] * flux[1] + j[2] * flux[2],
        ]
        energy = sum(flux[c] * fwd[c, :, lanes].astype(F32) for c in range(3))
        energy = jnp.sum(energy, axis=0, keepdims=True)
        dens = density[:, lanes]
        grad[:, lanes] = SIMP_POWER * dens * dens * energy / samples
        sub = iota((GE, CHUNK), 0).astype(jnp.int16)
        none = jnp.zeros((2 * samples, CHUNK), BF16)
        terms, hot = [], []
        for m in range(6):
            named = edge[m : m + 1, lanes]
            low = (named & (GE - 1)).astype(jnp.int16)
            high = lax.shift_right_logical(named, GE.bit_length() - 1)
            high = jnp.broadcast_to(high, (2 * samples, CHUNK)).astype(jnp.int16)
            hot.append(jnp.where(sub == low, BF16(1), BF16(0)))
            term = sum(maps[c, m : m + 1, :] * field[c] for c in range(3))
            term = jnp.concatenate(split(term), 0)
            terms.append(
                jnp.concatenate(
                    [jnp.where(high == jnp.int16(k), term, none) for k in range(extended // GE)], 0
                )
            )
        acc[...] += mul(jnp.concatenate(terms, 1), jnp.concatenate(hot, 1), NT)
        return carry

    chunks = edges // CHUNK
    lax.fori_loop(0, EARLY, element_chunk, 0)

    await_bytes(codes.at[w], recv.at[1])
    for other in w_peers:
        push(codes.at[w], codes.at[w], 5, z * GROUP + other, ax)
    await_bytes(mapped.at[pl.ds(0, GROUP - 1)], recv.at[2])
    asked = codes[w]
    rank = lax.rem(iota((ring * CAP, rows), 0), CAP)

    def by_row(value):
        return jnp.concatenate([value] * GB, 0)

    for other in range(GROUP):
        hits = [
            as_bf16(asked == (((z * GROUP + other) * CAP + rank) * QB + q).astype(F32))
            for q in range(QB)
        ]
        source = side_by_side(mapped[other])
        source = [by_row(source[q * samples : (q + 1) * samples]) for q in range(QB)]
        reply_out[other] = add_halves(
            mul(jnp.concatenate(hits, 1), jnp.concatenate(source, 0))
        )
    for other in z_peers:
        push(
            reply_out.at[:, pl.ds(other * CAP, CAP)],
            reply_in.at[:, at_me],
            6,
            other * GROUP + w,
            ax,
        )
    pltpu.make_async_copy(reply_out.at[:, at_me], reply_in.at[:, at_me], recv.at[6]).start()

    await_bytes(rotor_mid, recv.at[3])
    for other in w_peers:
        push(rotor_mid.at[other], rotor_in.at[w], 7, z * GROUP + other, ax)
    rotor_in[w] = rotor_mid[w]

    lax.fori_loop(EARLY, chunks, element_chunk, 0)
    sums = acc[...].reshape(extended // GE, 2, samples, GE)
    sums = sums[:, 0] + sums[:, 1]
    sums = jnp.concatenate([sums[k] for k in range(extended // GE)], 1)
    lower_out[...] = sums[:, edges:extended]
    lower_copy = transfer(lower_out, lower_in, 4, me, above)

    @pl.when(has_above)
    def _():
        lower_copy.start()


    local = jnp.concatenate(
        [sums[:, 0:rotor_start]]
        + [
            sums[:, rotor_start + b * GE : rotor_start + (b + 1) * GE]
            + PENALTY * rotor[b * samples : (b + 1) * samples]
            for b in range(GB)
        ],
        1,
    )
    arrivals[10].wait()
    adjoint[...] = table_dot(table_t[...], local)
    arrivals[11].wait()
    chosen = as_bf16(iota((rows, slots), 1) == slot_col)
    chosen = mul(back[...], chosen).astype(BF16)

    await_bytes(codes.at[pl.ds(0, GROUP - 1)], recv.at[5])
    listed_t = codes[...].reshape(slots, rows).T
    rank_t = lax.rem(iota((rows, slots), 1), CAP)
    takers, counts = [], []
    for q in range(QB):
        hit = listed_t == ((me * CAP + rank_t) * QB + q).astype(F32)
        hit = jnp.where(hit, F32(1), F32(0))
        folded = sum(hit[b * samples : (b + 1) * samples] for b in range(GB))
        takers.append(folded.astype(BF16))
        counts.append(jnp.sum(folded, axis=1, keepdims=True))
    takers, counts = jnp.concatenate(takers, 0), jnp.concatenate(counts, 0)
    counted = counts * mapped[w]
    await_bytes(rotor_in.at[pl.ds(0, GROUP - 1)], recv.at[7])
    arrived = add_halves(mul(takers, side_by_side(rotor_in[...].reshape(slots, GE))))
    stator_term = -PENALTY * dot3(arrived - counted, mortar[...], NT)
    stator_term = jnp.concatenate(
        [stator_term[q * samples : (q + 1) * samples] for q in range(QB)], 1
    )
    adjoint[:, face : face + QB * GE] += table_dot(table_t[...], stator_term)

    @pl.when(has_below)
    def _():
        lower_copy.wait_recv()
        adjoint[:, 0:face] += table_dot(table_t[...], lower_in[...])

    await_bytes(reply_in, recv.at[6])
    facing = mul(chosen, side_by_side(reply_in[...].reshape(slots, GE)))
    facing = add_halves(facing[:rows]) + facing[rows:, :GE]
    for b in range(GB):
        lanes = slice(rotor_start + b * GE, rotor_start + (b + 1) * GE)
        adjoint[:, lanes] += facing[b * samples : (b + 1) * samples]

    @pl.when(has_below)
    def _():
        upper_copy.wait_send()

    @pl.when(has_above)
    def _():
        lower_copy.wait_send()

    await_bytes(codes.at[0, pl.ds(0, (ring - 1) * CAP)], send.at[1])
    await_bytes(mapped.at[pl.ds(0, GROUP - 1)], send.at[2])
    await_bytes(rotor_mid.at[:, pl.ds(0, (ring - 1) * CAP)], send.at[3])
    await_bytes(codes.at[pl.ds(0, GROUP - 1)], send.at[5])
    await_bytes(reply_out.at[:, pl.ds(0, (ring - 1) * CAP)], send.at[6])
    await_bytes(rotor_in.at[pl.ds(0, GROUP - 1)], send.at[7])


def flush(adjoint, grad, adjoint_hbm, grad_hbm, sems):
    copies = (
        pltpu.make_async_copy(adjoint, adjoint_hbm, sems.at[0]),
        pltpu.make_async_copy(grad, grad_hbm, sems.at[1]),
    )
    for copy in copies:
        copy.start()
    for copy in copies:
        copy.wait()


def on_device(coeffs, elem_edge, curl_map, jacobian, flux_fwd, density, mortar, gap_peer, gap_block):
    stators, axials = lax.axis_size("stator"), lax.axis_size("axial")
    samples, edges = coeffs.shape
    elements = elem_edge.shape[1]
    face = edges // 8
    rows = samples * GB
    ring = stators // GROUP
    table = dft_table(samples)
    operands = (
        coeffs,
        elem_edge,
        curl_map,
        jacobian,
        flux_fwd,
        density.reshape(1, elements),
        mortar,
        gap_peer.reshape(1, rows),
        gap_block.reshape(1, rows),
        jnp.asarray(triple(table)),
        jnp.asarray(triple(np.ascontiguousarray(table.T))),
        jnp.asarray(back_table(table)),
    )
    vmem = pl.BlockSpec(memory_space=pltpu.VMEM)
    hbm = pl.BlockSpec(memory_space=pltpu.HBM)
    shapes = (
        jax.ShapeDtypeStruct((samples, edges), F32),
        jax.ShapeDtypeStruct((1, elements), F32),
    )
    strip = pltpu.VMEM((samples, face), F32)
    slotted = pltpu.VMEM((GROUP, ring * CAP, GE), F32)
    results = pl.pallas_call(
        functools.partial(kernel, stators, axials),
        out_shape=shapes,
        in_specs=[hbm] * len(operands),
        out_specs=(vmem, vmem),
        scratch_shapes=[pltpu.VMEM(operand.shape, operand.dtype) for operand in operands]
        + [
            strip,
            strip,
            strip,
            pltpu.VMEM((CAP, rows), F32),
            pltpu.VMEM((GROUP, ring * CAP, rows), F32),
            pltpu.VMEM((GROUP, samples * QB, GE), F32),
            slotted,
            slotted,
            slotted,
            slotted,
            slotted,
            pltpu.VMEM((samples, edges + face), F32),
            pltpu.VMEM((6, samples, elements), F32),
            pltpu.VMEM(((edges + face) // GE * 2 * samples, GE), F32),
            pltpu.SemaphoreType.DMA((len(operands),)),
            pltpu.SemaphoreType.DMA((8,)),
            pltpu.SemaphoreType.DMA((8,)),
        ],
        compiler_params=pltpu.CompilerParams(
            collective_id=0, has_side_effects=True, vmem_limit_bytes=32 * 1024 * 1024
        ),
    )(*(pltpu.with_memory_space_constraint(operand, pltpu.HBM) for operand in operands))
    adjoint, grad = pl.pallas_call(
        flush,
        out_shape=shapes,
        in_specs=[vmem, vmem],
        out_specs=(hbm, hbm),
        scratch_shapes=[pltpu.SemaphoreType.DMA((2,))],
    )(*(pltpu.with_memory_space_constraint(result, pltpu.VMEM) for result in results))
    return adjoint, grad.reshape(elements)


def solution(mesh):
    placed = (
        P(None, ("stator", "axial")),
        P(None, ("stator", "axial")),
        P(None, None, ("stator", "axial")),
        P(None, None, ("stator", "axial")),
        P(None, None, ("stator", "axial")),
        P(("stator", "axial")),
        P(),
        P(("stator", "axial"), None),
        P(("stator", "axial")),
    )
    return jax.shard_map(
        on_device,
        mesh=mesh,
        in_specs=placed,
        out_specs=(P(None, ("stator", "axial")), P(("stator", "axial"))),
        check_vma=False,
    )
```

```python
import functools
import math

import jax
import jax.numpy as jnp
import numpy as np
from jax import lax
from jax.experimental import pallas as pl
from jax.experimental.pallas import tpu as pltpu
from jax.sharding import PartitionSpec as P

GE = 128
GB = 4
QB = 2
CAP = 4
PENALTY = 4.0
SIMP_POWER = 3.0
CHUNK = 256
EARLY = 2
GROUP = 8

MESH = pl.DeviceIdType.MESH
F32 = jnp.float32
BF16 = jnp.bfloat16
NN = (((1,), (0,)), ((), ()))
NT = (((1,), (1,)), ((), ()))


def dft_table(count):
    rows = np.arange(count, dtype=np.float64)[:, None]
    index = np.arange(count)
    harmonic = ((index + 1) // 2).astype(np.float64)[None, :]
    is_sine = ((index % 2 == 0) & (index > 0))[None, :]
    angle = 2.0 * math.pi * harmonic * rows / count
    table = np.where(is_sine, np.sin(angle), np.cos(angle))
    return (table * math.sqrt(2.0 / count)).astype(np.float32)


def triple(table):
    high = table.astype(jnp.bfloat16)
    low = (table - high.astype(np.float32)).astype(jnp.bfloat16)
    return np.concatenate([high, high, low], 1)


def back_table(table):
    scaled = np.kron(np.eye(GB, dtype=np.float32), -PENALTY * table.T).astype(np.float32)
    high = scaled.astype(jnp.bfloat16)
    low = (scaled - high.astype(np.float32)).astype(jnp.bfloat16)
    return np.concatenate([high, low], 0)


def split(value):
    high = value.astype(BF16)
    return high, (value - high.astype(F32)).astype(BF16)


def mul(a, b, dims=NN):
    return lax.dot_general(a, b, dims, preferred_element_type=F32)


def table_dot(table, value):
    high, low = split(value)
    return mul(table, jnp.concatenate([high, low, high], 0))


def dot3(a, b, dims=NN):
    a_high, a_low = split(a)
    b_high, b_low = split(b)
    return mul(a_high, b_high, dims) + mul(a_high, b_low, dims) + mul(a_low, b_high, dims)


def side_by_side(value):
    return jnp.concatenate(split(value), 1)


def add_halves(value):
    half = value.shape[1] // 2
    return value[:, :half] + value[:, half:]


def as_bf16(mask):
    return jnp.where(mask, F32(1), F32(0)).astype(BF16)


def iota(shape, dim):
    return lax.broadcasted_iota(jnp.int32, shape, dim)


def kernel(
    stators,
    axials,
    coeffs_hbm,
    edge_hbm,
    curl_hbm,
    jac_hbm,
    fwd_hbm,
    density_hbm,
    mortar_hbm,
    peers_hbm,
    blocks_hbm,
    table_hbm,
    table_t_hbm,
    back_hbm,
    adjoint,
    grad,
    coeffs,
    edge,
    curl,
    jac,
    fwd,
    density,
    mortar,
    peers,
    blocks,
    table,
    table_t,
    back,
    upper,
    lower_out,
    lower_in,
    code_own,
    codes,
    mapped,
    rotor_out,
    rotor_mid,
    rotor_in,
    reply_out,
    reply_in,
    ext,
    values,
    acc,
    load,
    send,
    recv,
):
    samples, edges = coeffs.shape
    face = edges // 8
    extended = edges + face
    rows = samples * GB
    ring = stators // GROUP
    rotor_start = edges - GB * GE
    me, ax = lax.axis_index("stator"), lax.axis_index("axial")
    z, w = lax.div(me, GROUP), lax.rem(me, GROUP)
    above, below = lax.rem(ax + 1, axials), lax.rem(ax + axials - 1, axials)

    along_z = sorted(range(1, ring), key=lambda step: -min(step, ring - step))
    along_w = sorted(range(1, GROUP), key=lambda step: -min(step, GROUP - step))
    z_peers = [lax.rem(z + step, ring) for step in along_z]
    pairs = GROUP // 2
    w_peers = [
        lax.rem(lax.div(w, 2) + turn, pairs) * 2 + lax.rem(w + core, 2)
        for turn, core in ((2, 0), (2, 1), (1, 0), (3, 0), (1, 1), (3, 1), (0, 1))
    ]

    barrier = pltpu.get_barrier_semaphore()

    def greet(stator, axial):
        pl.semaphore_signal(barrier, inc=1, device_id=(stator, axial), device_id_type=MESH)

    for other in z_peers:
        greet(other * GROUP + w, ax)
    for other in w_peers:
        greet(z * GROUP + other, ax)
    has_above, has_below = ax < axials - 1, ax > 0

    @pl.when(has_above)
    def _():
        greet(me, above)

    @pl.when(has_below)
    def _():
        greet(me, below)


    arrivals = []
    for index, (source, target) in enumerate(
        (
            (peers_hbm, peers),
            (blocks_hbm, blocks),
            (coeffs_hbm, coeffs),
            (table_hbm, table),
            (mortar_hbm, mortar),
            (edge_hbm, edge),
            (curl_hbm, curl),
            (jac_hbm, jac),
            (fwd_hbm, fwd),
            (density_hbm, density),
            (table_t_hbm, table_t),
            (back_hbm, back),
        )
    ):
        arrivals.append(pltpu.make_async_copy(source, target, load.at[index]))
        arrivals[-1].start()

    def transfer(source, target, index, stator, axial):
        return pltpu.make_async_remote_copy(
            src_ref=source,
            dst_ref=target,
            send_sem=send.at[index],
            recv_sem=recv.at[index],
            device_id=(stator, axial),
            device_id_type=MESH,
        )

    def push(*where):
        transfer(*where).start()

    def await_bytes(view, sem):
        pltpu.make_async_copy(view, view, sem).wait()

    arrivals[2].wait()
    arrivals[3].wait()
    arrivals[4].wait()
    own = table_dot(table[...], coeffs[...])
    ext[:, 0:edges] = own
    faces = jnp.concatenate(
        [own[:, face + q * GE : face + (q + 1) * GE] for q in range(QB)], 0
    )
    own_mapped = dot3(faces, mortar[...])
    mapped[w] = own_mapped

    arrivals[0].wait()
    arrivals[1].wait()
    a, b = iota((rows, rows), 0), iota((rows, rows), 1)
    own_order = b == lax.rem(a, samples) * GB + lax.div(a, samples)
    listed = (peers[...] * QB + blocks[...]).astype(F32)
    col = jnp.sum(jnp.where(own_order, listed, 0.0), axis=1, keepdims=True)
    row = jnp.sum(jnp.where(a == b, col, 0.0), axis=0, keepdims=True)
    peer_col, peer_row = jnp.floor(col * 0.5), jnp.floor(row * 0.5)
    same = peer_col == peer_row
    rank_row = jnp.sum(jnp.where(same & (a < b), 1.0, 0.0), axis=0, keepdims=True)
    rank_col = jnp.sum(jnp.where(same & (b < a), 1.0, 0.0), axis=1, keepdims=True)

    def slot(peer, rank):
        ring_place = jnp.floor(peer * (1.0 / GROUP))
        group_place = peer - GROUP * ring_place
        return (group_place * (ring * CAP) + ring_place * CAP + rank).astype(jnp.int32)

    slot_row, slot_col = slot(peer_row, rank_row), slot(peer_col, rank_col)
    code_row = (peer_row * CAP + rank_row) * QB + (row - 2.0 * peer_row)
    code_own[...] = jnp.broadcast_to(code_row, (CAP, rows))

    slots = stators * CAP
    rotor = jnp.concatenate(
        [own[:, rotor_start + b * GE : rotor_start + (b + 1) * GE] for b in range(GB)], 0
    )
    placed = as_bf16(iota((slots, rows), 0) == slot_row)
    rotor_out[...] = add_halves(mul(placed, side_by_side(rotor))).reshape(rotor_out.shape)
    neighbours = jnp.where(has_above, 1, 0) + jnp.where(has_below, 1, 0)
    pl.semaphore_wait(barrier, (ring - 1) + (GROUP - 1) + neighbours)

    at_me = pl.ds(z * CAP, CAP)
    for other in z_peers:
        push(code_own, codes.at[w, at_me], 1, other * GROUP + w, ax)
    pltpu.make_async_copy(code_own, codes.at[w, at_me], recv.at[1]).start()
    upper_copy = transfer(coeffs.at[:, pl.ds(0, face)], upper, 0, me, below)

    @pl.when(has_below)
    def _():
        upper_copy.start()

    for other in w_peers:
        push(mapped.at[w], mapped.at[w], 2, z * GROUP + other, ax)
    for other in z_peers:
        push(
            rotor_out.at[:, pl.ds(other * CAP, CAP)],
            rotor_mid.at[:, at_me],
            3,
            other * GROUP + w,
            ax,
        )
    pltpu.make_async_copy(rotor_out.at[:, at_me], rotor_mid.at[:, at_me], recv.at[3]).start()

    arrivals[5].wait()

    def pick(lanes, m):
        named = jnp.broadcast_to(edge[m : m + 1, lanes], (samples, GE))
        return named & (GE - 1), lax.shift_right_logical(named, GE.bit_length() - 1)

    def gather_own(part, carry):
        lanes = pl.ds(pl.multiple_of(part * GE, GE), GE)
        for m in range(6):
            low, high = pick(lanes, m)
            found = None
            for k in range(edges // GE):
                here = jnp.take_along_axis(ext[:, k * GE : (k + 1) * GE], low, axis=1)
                found = here if found is None else jnp.where(high == k, here, found)
            values[m, :, lanes] = found
        return carry

    lax.fori_loop(0, edges // GE, gather_own, 0)

    @pl.when(has_above)
    def _():
        upper_copy.wait_recv()

    @pl.when(jnp.logical_not(has_above))
    def _():
        upper[...] = jnp.zeros_like(upper)

    ext[:, edges:extended] = table_dot(table[...], upper[...])
    for index in range(6, 10):
        arrivals[index].wait()
    acc[...] = jnp.zeros_like(acc)

    def element_chunk(chunk, carry):
        lanes = pl.ds(pl.multiple_of(chunk * CHUNK, CHUNK), CHUNK)
        found = []
        for m in range(6):
            pieces = []
            for part in range(CHUNK // GE):
                here = pl.ds(pl.multiple_of(chunk * CHUNK + part * GE, GE), GE)
                low, high = pick(here, m)
                rim = jnp.take_along_axis(ext[:, edges:extended], low, axis=1)
                pieces.append(jnp.where(high == edges // GE, rim, values[m, :, here]))
            found.append(jnp.concatenate(pieces, 1))
        maps = curl[:, :, lanes]
        flux = [sum(maps[c, m : m + 1, :] * found[m] for m in range(6)) for c in range(3)]
        j = [jac[k, :, lanes].astype(F32) for k in range(6)]
        field = [
            j[0] * flux[0] + j[3] * flux[1] + j[4] * flux[2],
            j[3] * flux[0] + j[1] * flux[1] + j[5] * flux[2],
            j[4] * flux[0] + j[5] * flux[1] + j[2] * flux[2],
        ]
        energy = sum(flux[c] * fwd[c, :, lanes].astype(F32) for c in range(3))
        energy = jnp.sum(energy, axis=0, keepdims=True)
        dens = density[:, lanes]
        grad[:, lanes] = SIMP_POWER * dens * dens * energy / samples
        sub = iota((GE, CHUNK), 0).astype(jnp.int16)
        none = jnp.zeros((2 * samples, CHUNK), BF16)
        terms, hot = [], []
        for m in range(6):
            named = edge[m : m + 1, lanes]
            low = (named & (GE - 1)).astype(jnp.int16)
            high = lax.shift_right_logical(named, GE.bit_length() - 1)
            high = jnp.broadcast_to(high, (2 * samples, CHUNK)).astype(jnp.int16)
            hot.append(jnp.where(sub == low, BF16(1), BF16(0)))
            term = sum(maps[c, m : m + 1, :] * field[c] for c in range(3))
            term = jnp.concatenate(split(term), 0)
            terms.append(
                jnp.concatenate(
                    [jnp.where(high == jnp.int16(k), term, none) for k in range(extended // GE)], 0
                )
            )
        acc[...] += mul(jnp.concatenate(terms, 1), jnp.concatenate(hot, 1), NT)
        return carry

    chunks = edges // CHUNK
    lax.fori_loop(0, EARLY, element_chunk, 0)

    await_bytes(codes.at[w], recv.at[1])
    for other in w_peers:
        push(codes.at[w], codes.at[w], 5, z * GROUP + other, ax)
    await_bytes(mapped.at[pl.ds(0, GROUP - 1)], recv.at[2])
    asked = codes[w]
    rank = lax.rem(iota((ring * CAP, rows), 0), CAP)

    def by_row(value):
        return jnp.concatenate([value] * GB, 0)

    for other in range(GROUP):
        hits = [
            as_bf16(asked == (((z * GROUP + other) * CAP + rank) * QB + q).astype(F32))
            for q in range(QB)
        ]
        source = side_by_side(mapped[other])
        source = [by_row(source[q * samples : (q + 1) * samples]) for q in range(QB)]
        reply_out[other] = add_halves(
            mul(jnp.concatenate(hits, 1), jnp.concatenate(source, 0))
        )
    for other in z_peers:
        push(
            reply_out.at[:, pl.ds(other * CAP, CAP)],
            reply_in.at[:, at_me],
            6,
            other * GROUP + w,
            ax,
        )
    pltpu.make_async_copy(reply_out.at[:, at_me], reply_in.at[:, at_me], recv.at[6]).start()

    await_bytes(rotor_mid, recv.at[3])
    for other in w_peers:
        push(rotor_mid.at[other], rotor_in.at[w], 7, z * GROUP + other, ax)
    rotor_in[w] = rotor_mid[w]

    lax.fori_loop(EARLY, chunks, element_chunk, 0)
    sums = acc[...].reshape(extended // GE, 2, samples, GE)
    sums = sums[:, 0] + sums[:, 1]
    sums = jnp.concatenate([sums[k] for k in range(extended // GE)], 1)
    lower_out[...] = sums[:, edges:extended]
    lower_copy = transfer(lower_out, lower_in, 4, me, above)

    @pl.when(has_above)
    def _():
        lower_copy.start()


    local = jnp.concatenate(
        [sums[:, 0:rotor_start]]
        + [
            sums[:, rotor_start + b * GE : rotor_start + (b + 1) * GE]
            + PENALTY * rotor[b * samples : (b + 1) * samples]
            for b in range(GB)
        ],
        1,
    )
    arrivals[10].wait()
    adjoint[...] = table_dot(table_t[...], local)
    arrivals[11].wait()
    chosen = as_bf16(iota((rows, slots), 1) == slot_col)
    chosen = mul(back[...], chosen).astype(BF16)

    await_bytes(codes.at[pl.ds(0, GROUP - 1)], recv.at[5])
    listed_t = codes[...].reshape(slots, rows).T
    rank_t = lax.rem(iota((rows, slots), 1), CAP)
    takers, counts = [], []
    for q in range(QB):
        hit = listed_t == ((me * CAP + rank_t) * QB + q).astype(F32)
        hit = jnp.where(hit, F32(1), F32(0))
        folded = sum(hit[b * samples : (b + 1) * samples] for b in range(GB))
        takers.append(folded.astype(BF16))
        counts.append(jnp.sum(folded, axis=1, keepdims=True))
    takers, counts = jnp.concatenate(takers, 0), jnp.concatenate(counts, 0)
    counted = PENALTY * dot3(counts * mapped[w], mortar[...], NT)
    counted = jnp.concatenate([counted[q * samples : (q + 1) * samples] for q in range(QB)], 1)
    adjoint[:, face : face + QB * GE] += table_dot(table_t[...], counted)
    wide = QB * samples
    taken = jnp.concatenate([back[0:wide, 0:wide], back[rows : rows + wide, 0:wide]], 0)
    taken = mul(taken, takers).astype(BF16)

    @pl.when(has_below)
    def _():
        lower_copy.wait_recv()
        adjoint[:, 0:face] += table_dot(table_t[...], lower_in[...])

    await_bytes(rotor_in.at[pl.ds(0, GROUP - 1)], recv.at[7])
    await_bytes(reply_in, recv.at[6])
    arrived = mul(taken, side_by_side(rotor_in[...].reshape(slots, GE)))
    arrived = add_halves(arrived[:wide]) + arrived[wide:, :GE]
    stator_term = dot3(arrived, mortar[...], NT)
    for q in range(QB):
        lanes = slice(face + q * GE, face + (q + 1) * GE)
        adjoint[:, lanes] += stator_term[q * samples : (q + 1) * samples]

    facing = mul(chosen, side_by_side(reply_in[...].reshape(slots, GE)))
    facing = add_halves(facing[:rows]) + facing[rows:, :GE]
    for b in range(GB):
        lanes = slice(rotor_start + b * GE, rotor_start + (b + 1) * GE)
        adjoint[:, lanes] += facing[b * samples : (b + 1) * samples]

    @pl.when(has_below)
    def _():
        upper_copy.wait_send()

    @pl.when(has_above)
    def _():
        lower_copy.wait_send()

    await_bytes(codes.at[0, pl.ds(0, (ring - 1) * CAP)], send.at[1])
    await_bytes(mapped.at[pl.ds(0, GROUP - 1)], send.at[2])
    await_bytes(rotor_mid.at[:, pl.ds(0, (ring - 1) * CAP)], send.at[3])
    await_bytes(codes.at[pl.ds(0, GROUP - 1)], send.at[5])
    await_bytes(reply_out.at[:, pl.ds(0, (ring - 1) * CAP)], send.at[6])
    await_bytes(rotor_in.at[pl.ds(0, GROUP - 1)], send.at[7])


def flush(adjoint, grad, adjoint_hbm, grad_hbm, sems):
    copies = (
        pltpu.make_async_copy(adjoint, adjoint_hbm, sems.at[0]),
        pltpu.make_async_copy(grad, grad_hbm, sems.at[1]),
    )
    for copy in copies:
        copy.start()
    for copy in copies:
        copy.wait()


def on_device(coeffs, elem_edge, curl_map, jacobian, flux_fwd, density, mortar, gap_peer, gap_block):
    stators, axials = lax.axis_size("stator"), lax.axis_size("axial")
    samples, edges = coeffs.shape
    elements = elem_edge.shape[1]
    face = edges // 8
    rows = samples * GB
    ring = stators // GROUP
    table = dft_table(samples)
    operands = (
        coeffs,
        elem_edge,
        curl_map,
        jacobian,
        flux_fwd,
        density.reshape(1, elements),
        mortar,
        gap_peer.reshape(1, rows),
        gap_block.reshape(1, rows),
        jnp.asarray(triple(table)),
        jnp.asarray(triple(np.ascontiguousarray(table.T))),
        jnp.asarray(back_table(table)),
    )
    vmem = pl.BlockSpec(memory_space=pltpu.VMEM)
    hbm = pl.BlockSpec(memory_space=pltpu.HBM)
    shapes = (
        jax.ShapeDtypeStruct((samples, edges), F32),
        jax.ShapeDtypeStruct((1, elements), F32),
    )
    strip = pltpu.VMEM((samples, face), F32)
    slotted = pltpu.VMEM((GROUP, ring * CAP, GE), F32)
    results = pl.pallas_call(
        functools.partial(kernel, stators, axials),
        out_shape=shapes,
        in_specs=[hbm] * len(operands),
        out_specs=(vmem, vmem),
        scratch_shapes=[pltpu.VMEM(operand.shape, operand.dtype) for operand in operands]
        + [
            strip,
            strip,
            strip,
            pltpu.VMEM((CAP, rows), F32),
            pltpu.VMEM((GROUP, ring * CAP, rows), F32),
            pltpu.VMEM((GROUP, samples * QB, GE), F32),
            slotted,
            slotted,
            slotted,
            slotted,
            slotted,
            pltpu.VMEM((samples, edges + face), F32),
            pltpu.VMEM((6, samples, elements), F32),
            pltpu.VMEM(((edges + face) // GE * 2 * samples, GE), F32),
            pltpu.SemaphoreType.DMA((len(operands),)),
            pltpu.SemaphoreType.DMA((8,)),
            pltpu.SemaphoreType.DMA((8,)),
        ],
        compiler_params=pltpu.CompilerParams(
            collective_id=0, has_side_effects=True, vmem_limit_bytes=32 * 1024 * 1024
        ),
    )(*(pltpu.with_memory_space_constraint(operand, pltpu.HBM) for operand in operands))
    adjoint, grad = pl.pallas_call(
        flush,
        out_shape=shapes,
        in_specs=[vmem, vmem],
        out_specs=(hbm, hbm),
        scratch_shapes=[pltpu.SemaphoreType.DMA((2,))],
    )(*(pltpu.with_memory_space_constraint(result, pltpu.VMEM) for result in results))
    return adjoint, grad.reshape(elements)


def solution(mesh):
    placed = (
        P(None, ("stator", "axial")),
        P(None, ("stator", "axial")),
        P(None, None, ("stator", "axial")),
        P(None, None, ("stator", "axial")),
        P(None, None, ("stator", "axial")),
        P(("stator", "axial")),
        P(),
        P(("stator", "axial"), None),
        P(("stator", "axial")),
    )
    return jax.shard_map(
        on_device,
        mesh=mesh,
        in_specs=placed,
        out_specs=(P(None, ("stator", "axial")), P(("stator", "axial"))),
        check_vma=False,
    )
```

```python
import functools
import math

import jax
import jax.numpy as jnp
import numpy as np
from jax import lax
from jax.experimental import pallas as pl
from jax.experimental.pallas import tpu as pltpu
from jax.sharding import PartitionSpec as P

GE = 128
GB = 4
QB = 2
CAP = 4
PENALTY = 4.0
SIMP_POWER = 3.0
CHUNK = 256
EARLY = 1
GROUP = 8

MESH = pl.DeviceIdType.MESH
F32 = jnp.float32
BF16 = jnp.bfloat16
NN = (((1,), (0,)), ((), ()))
NT = (((1,), (1,)), ((), ()))


def dft_table(count):
    rows = np.arange(count, dtype=np.float64)[:, None]
    index = np.arange(count)
    harmonic = ((index + 1) // 2).astype(np.float64)[None, :]
    is_sine = ((index % 2 == 0) & (index > 0))[None, :]
    angle = 2.0 * math.pi * harmonic * rows / count
    table = np.where(is_sine, np.sin(angle), np.cos(angle))
    return (table * math.sqrt(2.0 / count)).astype(np.float32)


def triple(table):
    high = table.astype(jnp.bfloat16)
    low = (table - high.astype(np.float32)).astype(jnp.bfloat16)
    return np.concatenate([high, high, low], 1)


def back_table(table):
    scaled = np.kron(np.eye(GB, dtype=np.float32), -PENALTY * table.T).astype(np.float32)
    high = scaled.astype(jnp.bfloat16)
    low = (scaled - high.astype(np.float32)).astype(jnp.bfloat16)
    return np.concatenate([high, low], 0)


def split(value):
    high = value.astype(BF16)
    return high, (value - high.astype(F32)).astype(BF16)


def mul(a, b, dims=NN):
    return lax.dot_general(a, b, dims, preferred_element_type=F32)


def table_dot(table, value):
    high, low = split(value)
    return mul(table, jnp.concatenate([high, low, high], 0))


def dot3(a, b, dims=NN):
    a_high, a_low = split(a)
    b_high, b_low = split(b)
    return mul(a_high, b_high, dims) + mul(a_high, b_low, dims) + mul(a_low, b_high, dims)


def side_by_side(value):
    return jnp.concatenate(split(value), 1)


def add_halves(value):
    half = value.shape[1] // 2
    return value[:, :half] + value[:, half:]


def as_bf16(mask):
    return jnp.where(mask, F32(1), F32(0)).astype(BF16)


def iota(shape, dim):
    return lax.broadcasted_iota(jnp.int32, shape, dim)


def kernel(
    stators,
    axials,
    coeffs_hbm,
    edge_hbm,
    curl_hbm,
    jac_hbm,
    fwd_hbm,
    density_hbm,
    mortar_hbm,
    peers_hbm,
    blocks_hbm,
    table_hbm,
    table_t_hbm,
    back_hbm,
    adjoint,
    grad,
    coeffs,
    edge,
    curl,
    jac,
    fwd,
    density,
    mortar,
    peers,
    blocks,
    table,
    table_t,
    back,
    upper,
    lower_out,
    lower_in,
    code_own,
    codes,
    mapped,
    rotor_out,
    rotor_mid,
    rotor_in,
    reply_out,
    reply_in,
    ext,
    values,
    acc,
    load,
    send,
    recv,
):
    samples, edges = coeffs.shape
    face = edges // 8
    extended = edges + face
    rows = samples * GB
    ring = stators // GROUP
    rotor_start = edges - GB * GE
    me, ax = lax.axis_index("stator"), lax.axis_index("axial")
    z, w = lax.div(me, GROUP), lax.rem(me, GROUP)
    above, below = lax.rem(ax + 1, axials), lax.rem(ax + axials - 1, axials)

    along_z = sorted(range(1, ring), key=lambda step: -min(step, ring - step))
    along_w = sorted(range(1, GROUP), key=lambda step: -min(step, GROUP - step))
    z_peers = [lax.rem(z + step, ring) for step in along_z]
    pairs = GROUP // 2
    w_peers = [
        lax.rem(lax.div(w, 2) + turn, pairs) * 2 + lax.rem(w + core, 2)
        for turn, core in ((2, 0), (2, 1), (1, 0), (3, 0), (1, 1), (3, 1), (0, 1))
    ]

    barrier = pltpu.get_barrier_semaphore()

    def greet(stator, axial):
        pl.semaphore_signal(barrier, inc=1, device_id=(stator, axial), device_id_type=MESH)

    for other in z_peers:
        greet(other * GROUP + w, ax)
    for other in w_peers:
        greet(z * GROUP + other, ax)
    has_above, has_below = ax < axials - 1, ax > 0

    @pl.when(has_above)
    def _():
        greet(me, above)

    @pl.when(has_below)
    def _():
        greet(me, below)


    arrivals = []
    for index, (source, target) in enumerate(
        (
            (peers_hbm, peers),
            (blocks_hbm, blocks),
            (coeffs_hbm, coeffs),
            (table_hbm, table),
            (mortar_hbm, mortar),
            (edge_hbm, edge),
            (curl_hbm, curl),
            (jac_hbm, jac),
            (fwd_hbm, fwd),
            (density_hbm, density),
            (table_t_hbm, table_t),
            (back_hbm, back),
        )
    ):
        arrivals.append(pltpu.make_async_copy(source, target, load.at[index]))
        arrivals[-1].start()

    def transfer(source, target, index, stator, axial):
        return pltpu.make_async_remote_copy(
            src_ref=source,
            dst_ref=target,
            send_sem=send.at[index],
            recv_sem=recv.at[index],
            device_id=(stator, axial),
            device_id_type=MESH,
        )

    def push(*where):
        transfer(*where).start()

    def await_bytes(view, sem):
        pltpu.make_async_copy(view, view, sem).wait()

    arrivals[2].wait()
    arrivals[3].wait()
    arrivals[4].wait()
    own = table_dot(table[...], coeffs[...])
    ext[:, 0:edges] = own
    faces = jnp.concatenate(
        [own[:, face + q * GE : face + (q + 1) * GE] for q in range(QB)], 0
    )
    own_mapped = dot3(faces, mortar[...])
    mapped[w] = own_mapped

    arrivals[0].wait()
    arrivals[1].wait()
    a, b = iota((rows, rows), 0), iota((rows, rows), 1)
    own_order = b == lax.rem(a, samples) * GB + lax.div(a, samples)
    listed = (peers[...] * QB + blocks[...]).astype(F32)
    col = jnp.sum(jnp.where(own_order, listed, 0.0), axis=1, keepdims=True)
    row = jnp.sum(jnp.where(a == b, col, 0.0), axis=0, keepdims=True)
    peer_col, peer_row = jnp.floor(col * 0.5), jnp.floor(row * 0.5)
    same = peer_col == peer_row
    rank_row = jnp.sum(jnp.where(same & (a < b), 1.0, 0.0), axis=0, keepdims=True)
    rank_col = jnp.sum(jnp.where(same & (b < a), 1.0, 0.0), axis=1, keepdims=True)

    def slot(peer, rank):
        ring_place = jnp.floor(peer * (1.0 / GROUP))
        group_place = peer - GROUP * ring_place
        return (group_place * (ring * CAP) + ring_place * CAP + rank).astype(jnp.int32)

    slot_row, slot_col = slot(peer_row, rank_row), slot(peer_col, rank_col)
    code_row = (peer_row * CAP + rank_row) * QB + (row - 2.0 * peer_row)
    code_own[...] = jnp.broadcast_to(code_row, (CAP, rows))

    slots = stators * CAP
    rotor = jnp.concatenate(
        [own[:, rotor_start + b * GE : rotor_start + (b + 1) * GE] for b in range(GB)], 0
    )
    placed = as_bf16(iota((slots, rows), 0) == slot_row)
    rotor_out[...] = add_halves(mul(placed, side_by_side(rotor))).reshape(rotor_out.shape)
    neighbours = jnp.where(has_above, 1, 0) + jnp.where(has_below, 1, 0)
    pl.semaphore_wait(barrier, (ring - 1) + (GROUP - 1) + neighbours)

    at_me = pl.ds(z * CAP, CAP)
    for other in z_peers:
        push(code_own, codes.at[w, at_me], 1, other * GROUP + w, ax)
    pltpu.make_async_copy(code_own, codes.at[w, at_me], recv.at[1]).start()
    upper_copy = transfer(coeffs.at[:, pl.ds(0, face)], upper, 0, me, below)

    @pl.when(has_below)
    def _():
        upper_copy.start()

    for other in w_peers:
        push(mapped.at[w], mapped.at[w], 2, z * GROUP + other, ax)
    for other in z_peers:
        push(
            rotor_out.at[:, pl.ds(other * CAP, CAP)],
            rotor_mid.at[:, at_me],
            3,
            other * GROUP + w,
            ax,
        )
    pltpu.make_async_copy(rotor_out.at[:, at_me], rotor_mid.at[:, at_me], recv.at[3]).start()

    arrivals[5].wait()

    def pick(lanes, m):
        named = jnp.broadcast_to(edge[m : m + 1, lanes], (samples, GE))
        return named & (GE - 1), lax.shift_right_logical(named, GE.bit_length() - 1)

    def gather_own(part, carry):
        lanes = pl.ds(pl.multiple_of(part * GE, GE), GE)
        for m in range(6):
            low, high = pick(lanes, m)
            found = None
            for k in range(edges // GE):
                here = jnp.take_along_axis(ext[:, k * GE : (k + 1) * GE], low, axis=1)
                found = here if found is None else jnp.where(high == k, here, found)
            values[m, :, lanes] = found
        return carry

    lax.fori_loop(0, edges // GE, gather_own, 0)

    @pl.when(has_above)
    def _():
        upper_copy.wait_recv()

    @pl.when(jnp.logical_not(has_above))
    def _():
        upper[...] = jnp.zeros_like(upper)

    ext[:, edges:extended] = table_dot(table[...], upper[...])
    for index in range(6, 10):
        arrivals[index].wait()
    acc[...] = jnp.zeros_like(acc)

    def element_chunk(chunk, carry):
        lanes = pl.ds(pl.multiple_of(chunk * CHUNK, CHUNK), CHUNK)
        found = []
        for m in range(6):
            pieces = []
            for part in range(CHUNK // GE):
                here = pl.ds(pl.multiple_of(chunk * CHUNK + part * GE, GE), GE)
                low, high = pick(here, m)
                rim = jnp.take_along_axis(ext[:, edges:extended], low, axis=1)
                pieces.append(jnp.where(high == edges // GE, rim, values[m, :, here]))
            found.append(jnp.concatenate(pieces, 1))
        maps = curl[:, :, lanes]
        flux = [sum(maps[c, m : m + 1, :] * found[m] for m in range(6)) for c in range(3)]
        j = [jac[k, :, lanes].astype(F32) for k in range(6)]
        field = [
            j[0] * flux[0] + j[3] * flux[1] + j[4] * flux[2],
            j[3] * flux[0] + j[1] * flux[1] + j[5] * flux[2],
            j[4] * flux[0] + j[5] * flux[1] + j[2] * flux[2],
        ]
        energy = sum(flux[c] * fwd[c, :, lanes].astype(F32) for c in range(3))
        energy = jnp.sum(energy, axis=0, keepdims=True)
        dens = density[:, lanes]
        grad[:, lanes] = SIMP_POWER * dens * dens * energy / samples
        sub = iota((GE, CHUNK), 0).astype(jnp.int16)
        none = jnp.zeros((2 * samples, CHUNK), BF16)
        terms, hot = [], []
        for m in range(6):
            named = edge[m : m + 1, lanes]
            low = (named & (GE - 1)).astype(jnp.int16)
            high = lax.shift_right_logical(named, GE.bit_length() - 1)
            high = jnp.broadcast_to(high, (2 * samples, CHUNK)).astype(jnp.int16)
            hot.append(jnp.where(sub == low, BF16(1), BF16(0)))
            term = sum(maps[c, m : m + 1, :] * field[c] for c in range(3))
            term = jnp.concatenate(split(term), 0)
            terms.append(
                jnp.concatenate(
                    [jnp.where(high == jnp.int16(k), term, none) for k in range(extended // GE)], 0
                )
            )
        acc[...] += mul(jnp.concatenate(terms, 1), jnp.concatenate(hot, 1), NT)
        return carry

    chunks = edges // CHUNK
    lax.fori_loop(0, EARLY, element_chunk, 0)

    await_bytes(codes.at[w], recv.at[1])
    for other in w_peers:
        push(codes.at[w], codes.at[w], 5, z * GROUP + other, ax)
    await_bytes(mapped.at[pl.ds(0, GROUP - 1)], recv.at[2])
    asked = codes[w]
    rank = lax.rem(iota((ring * CAP, rows), 0), CAP)

    def by_row(value):
        return jnp.concatenate([value] * GB, 0)

    for other in range(GROUP):
        hits = [
            as_bf16(asked == (((z * GROUP + other) * CAP + rank) * QB + q).astype(F32))
            for q in range(QB)
        ]
        source = side_by_side(mapped[other])
        source = [by_row(source[q * samples : (q + 1) * samples]) for q in range(QB)]
        reply_out[other] = add_halves(
            mul(jnp.concatenate(hits, 1), jnp.concatenate(source, 0))
        )
    for other in z_peers:
        push(
            reply_out.at[:, pl.ds(other * CAP, CAP)],
            reply_in.at[:, at_me],
            6,
            other * GROUP + w,
            ax,
        )
    pltpu.make_async_copy(reply_out.at[:, at_me], reply_in.at[:, at_me], recv.at[6]).start()

    await_bytes(rotor_mid, recv.at[3])
    for other in w_peers:
        push(rotor_mid.at[other], rotor_in.at[w], 7, z * GROUP + other, ax)
    rotor_in[w] = rotor_mid[w]

    lax.fori_loop(EARLY, chunks, element_chunk, 0)
    sums = acc[...].reshape(extended // GE, 2, samples, GE)
    sums = sums[:, 0] + sums[:, 1]
    sums = jnp.concatenate([sums[k] for k in range(extended // GE)], 1)
    lower_out[...] = sums[:, edges:extended]
    lower_copy = transfer(lower_out, lower_in, 4, me, above)

    @pl.when(has_above)
    def _():
        lower_copy.start()


    local = jnp.concatenate(
        [sums[:, 0:rotor_start]]
        + [
            sums[:, rotor_start + b * GE : rotor_start + (b + 1) * GE]
            + PENALTY * rotor[b * samples : (b + 1) * samples]
            for b in range(GB)
        ],
        1,
    )
    arrivals[10].wait()
    adjoint[...] = table_dot(table_t[...], local)
    arrivals[11].wait()
    chosen = as_bf16(iota((rows, slots), 1) == slot_col)
    chosen = mul(back[...], chosen).astype(BF16)

    await_bytes(codes.at[pl.ds(0, GROUP - 1)], recv.at[5])
    listed_t = codes[...].reshape(slots, rows).T
    rank_t = lax.rem(iota((rows, slots), 1), CAP)
    takers, counts = [], []
    for q in range(QB):
        hit = listed_t == ((me * CAP + rank_t) * QB + q).astype(F32)
        hit = jnp.where(hit, F32(1), F32(0))
        folded = sum(hit[b * samples : (b + 1) * samples] for b in range(GB))
        takers.append(folded.astype(BF16))
        counts.append(jnp.sum(folded, axis=1, keepdims=True))
    takers, counts = jnp.concatenate(takers, 0), jnp.concatenate(counts, 0)
    counted = PENALTY * dot3(counts * mapped[w], mortar[...], NT)
    counted = jnp.concatenate([counted[q * samples : (q + 1) * samples] for q in range(QB)], 1)
    adjoint[:, face : face + QB * GE] += table_dot(table_t[...], counted)
    wide = QB * samples
    taken = jnp.concatenate([back[0:wide, 0:wide], back[rows : rows + wide, 0:wide]], 0)
    taken = mul(taken, takers).astype(BF16)

    @pl.when(has_below)
    def _():
        lower_copy.wait_recv()

    @pl.when(jnp.logical_not(has_below))
    def _():
        lower_in[...] = jnp.zeros_like(lower_in)

    await_bytes(rotor_in.at[pl.ds(0, GROUP - 1)], recv.at[7])
    await_bytes(reply_in, recv.at[6])
    adjoint[:, 0:face] += table_dot(table_t[...], lower_in[...])
    arrived = mul(taken, side_by_side(rotor_in[...].reshape(slots, GE)))
    arrived = add_halves(arrived[:wide]) + arrived[wide:, :GE]
    stator_term = dot3(arrived, mortar[...], NT)
    for q in range(QB):
        lanes = slice(face + q * GE, face + (q + 1) * GE)
        adjoint[:, lanes] += stator_term[q * samples : (q + 1) * samples]

    facing = mul(chosen, side_by_side(reply_in[...].reshape(slots, GE)))
    facing = add_halves(facing[:rows]) + facing[rows:, :GE]
    for b in range(GB):
        lanes = slice(rotor_start + b * GE, rotor_start + (b + 1) * GE)
        adjoint[:, lanes] += facing[b * samples : (b + 1) * samples]

    @pl.when(has_below)
    def _():
        upper_copy.wait_send()

    @pl.when(has_above)
    def _():
        lower_copy.wait_send()

    await_bytes(codes.at[0, pl.ds(0, (ring - 1) * CAP)], send.at[1])
    await_bytes(mapped.at[pl.ds(0, GROUP - 1)], send.at[2])
    await_bytes(rotor_mid.at[:, pl.ds(0, (ring - 1) * CAP)], send.at[3])
    await_bytes(codes.at[pl.ds(0, GROUP - 1)], send.at[5])
    await_bytes(reply_out.at[:, pl.ds(0, (ring - 1) * CAP)], send.at[6])
    await_bytes(rotor_in.at[pl.ds(0, GROUP - 1)], send.at[7])


def flush(adjoint, grad, adjoint_hbm, grad_hbm, sems):
    copies = (
        pltpu.make_async_copy(adjoint, adjoint_hbm, sems.at[0]),
        pltpu.make_async_copy(grad, grad_hbm, sems.at[1]),
    )
    for copy in copies:
        copy.start()
    for copy in copies:
        copy.wait()


def on_device(coeffs, elem_edge, curl_map, jacobian, flux_fwd, density, mortar, gap_peer, gap_block):
    stators, axials = lax.axis_size("stator"), lax.axis_size("axial")
    samples, edges = coeffs.shape
    elements = elem_edge.shape[1]
    face = edges // 8
    rows = samples * GB
    ring = stators // GROUP
    table = dft_table(samples)
    operands = (
        coeffs,
        elem_edge,
        curl_map,
        jacobian,
        flux_fwd,
        density.reshape(1, elements),
        mortar,
        gap_peer.reshape(1, rows),
        gap_block.reshape(1, rows),
        jnp.asarray(triple(table)),
        jnp.asarray(triple(np.ascontiguousarray(table.T))),
        jnp.asarray(back_table(table)),
    )
    vmem = pl.BlockSpec(memory_space=pltpu.VMEM)
    hbm = pl.BlockSpec(memory_space=pltpu.HBM)
    shapes = (
        jax.ShapeDtypeStruct((samples, edges), F32),
        jax.ShapeDtypeStruct((1, elements), F32),
    )
    strip = pltpu.VMEM((samples, face), F32)
    slotted = pltpu.VMEM((GROUP, ring * CAP, GE), F32)
    results = pl.pallas_call(
        functools.partial(kernel, stators, axials),
        out_shape=shapes,
        in_specs=[hbm] * len(operands),
        out_specs=(vmem, vmem),
        scratch_shapes=[pltpu.VMEM(operand.shape, operand.dtype) for operand in operands]
        + [
            strip,
            strip,
            strip,
            pltpu.VMEM((CAP, rows), F32),
            pltpu.VMEM((GROUP, ring * CAP, rows), F32),
            pltpu.VMEM((GROUP, samples * QB, GE), F32),
            slotted,
            slotted,
            slotted,
            slotted,
            slotted,
            pltpu.VMEM((samples, edges + face), F32),
            pltpu.VMEM((6, samples, elements), F32),
            pltpu.VMEM(((edges + face) // GE * 2 * samples, GE), F32),
            pltpu.SemaphoreType.DMA((len(operands),)),
            pltpu.SemaphoreType.DMA((8,)),
            pltpu.SemaphoreType.DMA((8,)),
        ],
        compiler_params=pltpu.CompilerParams(
            collective_id=0, has_side_effects=True, vmem_limit_bytes=32 * 1024 * 1024
        ),
    )(*(pltpu.with_memory_space_constraint(operand, pltpu.HBM) for operand in operands))
    adjoint, grad = pl.pallas_call(
        flush,
        out_shape=shapes,
        in_specs=[vmem, vmem],
        out_specs=(hbm, hbm),
        scratch_shapes=[pltpu.SemaphoreType.DMA((2,))],
    )(*(pltpu.with_memory_space_constraint(result, pltpu.VMEM) for result in results))
    return adjoint, grad.reshape(elements)


def solution(mesh):
    placed = (
        P(None, ("stator", "axial")),
        P(None, ("stator", "axial")),
        P(None, None, ("stator", "axial")),
        P(None, None, ("stator", "axial")),
        P(None, None, ("stator", "axial")),
        P(("stator", "axial")),
        P(),
        P(("stator", "axial"), None),
        P(("stator", "axial")),
    )
    return jax.shard_map(
        on_device,
        mesh=mesh,
        in_specs=placed,
        out_specs=(P(None, ("stator", "axial")), P(("stator", "axial"))),
        check_vma=False,
    )
```
